128 devices in a mesh: wide: 16 (over x, y), narrow: 8 (over z, core).
Axes of the slice: x: 4, y: 4, z: 4, core: 2. Of those that a mesh axis runs over, the one named last changes fastest.
Arguments:
- features: bfloat16 [16, 8, 8, 48, 9216], P('wide', 'narrow'), may hold values from -6 to 6
- patch_ids: int32 [16, 8, 8], P('wide', 'narrow'), may hold values from 0 to 991, as said below
- patch_count: int32 [16, 8], P('wide', 'narrow'), may hold values from 6 to 8, as said below
- labels: int32 [1536, 1536], P('wide', 'narrow'), may hold values from 0 to 117
- mlp_weight: bfloat16 [48, 48], replicated, may hold values from -0.875 to 0.875
- mlp_bias: float32 [48], replicated, may hold values from -3 to 3
- out_weight: bfloat16 [118, 48], replicated
- out_bias: float32 [118], replicated, may hold values from -4 to 4
Outputs:
- blended: bfloat16 [118, 1536, 1536], P(None, 'wide', 'narrow')
- dice: float32 [118], replicated
- slab_sums: float32 [16, 8, 2, 118], P('wide', 'narrow')
The draws below stay inside these ranges and needn't reach their ends.
Inputs may be any that keep to these rules, and one draw needn't show every extreme that they name: `patch_ids`: each device lists patches whose start quadrant row lies in its own band of 4 rows along y (at most 1536 / 48 - 2); the start columns of one device's listed patches share one parity and are pairwise more than one apart, so one device sends at most 4 quadrants to one x slab; entries beyond the count are arbitrary ids. `patch_count`: some device lists 8 patches.
All inputs are finite; a program needn't handle non-finite values.
Results may differ from the reference program's by a relative error of at most 0.0035.
The reference program's roundings to bfloat16 on the way (of `active` and `weighted`) count: a program that leaves them out, or rounds other values in their place, can miss the bound.
Values may be sent and summed in bfloat16 or wider, within the bound.
No kernel may reach another device: no remote copies, remote signals or barrier semaphores. Data moves between devices by JAX's collectives and lax.ppermute only.
A program may use at most 192 MiB of HBM per device.

```python
import jax
import jax.numpy as jnp
from jax import lax

FEAT = 48
CLASSES = 118
PATCH = 96
SY = 192
SX = 96
PSLOT = 8
NX = 1536
NY = 1536
N_WIDE = 16
N_NARROW = 8


def layout(key):
    keys = jax.random.split(key, 5)
    devices = N_WIDE * N_NARROW
    flat = jnp.arange(devices, dtype=jnp.int32).reshape(N_WIDE, N_NARROW)
    chosen_dev = jax.random.randint(keys[0], (), 0, devices)
    parity = jax.random.randint(keys[1], (N_WIDE, N_NARROW), 0, 2)
    count = jax.random.randint(keys[2], (N_WIDE, N_NARROW), PSLOT - PSLOT // 4, PSLOT + 1)
    count = jnp.where(flat == chosen_dev, PSLOT, count)
    cand = jnp.arange(N_WIDE, dtype=jnp.int32)
    rank = jax.random.randint(keys[3], (N_WIDE, N_NARROW, N_WIDE), 0, 4096) * N_WIDE + cand
    barred = (parity[:, :, None] == 1) & (cand[None, None, :] == N_WIDE - 1)
    rank = jnp.where(barred, rank + 4096 * N_WIDE, rank)
    order = jnp.argsort(rank, axis=-1, stable=True).astype(jnp.int32)[:, :, :PSLOT]
    column = jnp.minimum(2 * order + parity[:, :, None], 2 * N_WIDE - 2)
    quad = PATCH // 2
    rows_q = NY // quad
    band = SY // quad
    base = jnp.arange(N_NARROW, dtype=jnp.int32)[None, :, None] * band
    row = base + jax.random.randint(keys[4], (N_WIDE, N_NARROW, PSLOT), 0, band)
    row = jnp.minimum(row, rows_q - 2)
    ids = column * rows_q + row
    return (ids.astype(jnp.int32), count.astype(jnp.int32))


def draw_patch_ids(key, part):
    ids, count = layout(key)
    return ids


def draw_patch_count(key, part):
    ids, count = layout(key)
    return count


def draw_labels(key, part):
    key = jax.random.fold_in(key, 7)
    coarse = jax.random.randint(key, (NX // 4, NY // 4), 0, CLASSES)
    return jnp.repeat(jnp.repeat(coarse, 4, axis=0), 4, axis=1).astype(jnp.int32)


def draw_out_weight(key, part):
    key = jax.random.fold_in(key, 11)
    first = jax.random.fold_in(key, 0)
    base = jax.random.normal(first, (CLASSES, FEAT), jnp.float32) / jnp.sqrt(jnp.float32(FEAT))
    return base.astype(jnp.bfloat16)


def block_levels(rng, shape, pieces, smallest, largest):
    def one(axis_at, parts):
        steps = jax.random.uniform(jax.random.fold_in(jax.random.fold_in(rng, 6), axis_at), (parts,), jnp.float32, smallest / len(pieces), largest / len(pieces))
        return jnp.repeat(jnp.exp(steps), shape[axis_at] // parts).reshape((-1,) + (1,) * (len(shape) - axis_at - 1))

    factor_of = one(*pieces[0])
    for cut in pieces[1:]:
        factor_of = factor_of * one(*cut)
    return factor_of


def scatter_about(stream_key, dims, deviation, reach, cuts=(), kind=jnp.bfloat16):
    drawn = jax.random.normal(stream_key, dims, jnp.float32) * deviation
    if len(cuts) > 0:
        drawn = block_levels(stream_key, dims, cuts, -0.22, 0.18) * drawn
    return jnp.clip(drawn, min=-reach, max=reach).astype(kind)


def setup_inputs(seed: int = 0) -> dict:
    seeds = jax.random.split(jax.random.key(seed), 9)
    features = scatter_about(seeds[0], (N_WIDE, N_NARROW, PSLOT, FEAT, PATCH * PATCH), 1.0, 6.0, ((0, 16), (1, 8)))
    patch_ids = draw_patch_ids(jax.random.fold_in(seeds[8], 71), 0)
    patch_count = draw_patch_count(jax.random.fold_in(seeds[8], 71), 0)
    labels = draw_labels(jax.random.fold_in(seeds[8], 71), 0)
    mlp_weight = scatter_about(seeds[4], (FEAT, FEAT), FEAT ** -0.5, 0.875)
    mlp_bias = scatter_about(seeds[5], (FEAT,), 0.5, 3.0, (), jnp.float32)
    out_weight = draw_out_weight(jax.random.fold_in(seeds[8], 71), 0)
    out_bias = scatter_about(seeds[7], (CLASSES,), 1.0, 4.0, (), jnp.float32)
    return {"features": features, "patch_ids": patch_ids, "patch_count": patch_count, "labels": labels, "mlp_weight": mlp_weight, "mlp_bias": mlp_bias, "out_weight": out_weight, "out_bias": out_bias}


def gauss_table(size):
    axis_pos = jnp.arange(size, dtype=jnp.float32) - (size - 1) / 2.0
    sigma = 0.125 * size
    squared = axis_pos[:, None] * axis_pos[:, None] + axis_pos[None, :] * axis_pos[None, :]
    return jnp.exp(-squared / (2.0 * sigma * sigma)).reshape(size * size)


def patch_head(feats, mlp_weight, mlp_bias, out_weight, out_bias, gauss):
    hidden = jnp.einsum('oc,kcv->kov', mlp_weight.astype(jnp.float32), feats.astype(jnp.float32))
    active = (feats.astype(jnp.float32) + jax.nn.relu(hidden + mlp_bias[None, :, None])).astype(jnp.bfloat16)
    logits = jnp.einsum('oc,kcv->kov', out_weight.astype(jnp.float32), active.astype(jnp.float32))
    probs = jax.nn.softmax(logits + out_bias[None, :, None], axis=-2)
    return (probs * gauss[None, None, :]).astype(jnp.bfloat16)


def edge_of(field):
    padded = jnp.pad(field, 1)
    low = jnp.minimum(jnp.minimum(padded[:-2, 1:-1], padded[2:, 1:-1]), jnp.minimum(padded[1:-1, :-2], padded[1:-1, 2:]))
    return field - jnp.minimum(field, low)


def spread_of(field):
    padded = jnp.pad(field, 1)
    high = jnp.maximum(jnp.maximum(padded[:-2, 1:-1], padded[2:, 1:-1]), jnp.maximum(padded[1:-1, :-2], padded[1:-1, 2:]))
    return jnp.maximum(field, high)


def slab_total(field):
    return jnp.sum(field.reshape(N_WIDE, SX, N_NARROW, SY), axis=(1, 3))


def reference(features, patch_ids, patch_count, labels, mlp_weight, mlp_bias, out_weight, out_bias):
    quad = PATCH // 2
    rows_q = NY // quad
    gauss = gauss_table(PATCH)
    gauss_square = gauss.reshape(PATCH, PATCH)
    total0 = jnp.zeros((CLASSES, NX, NY), jnp.float32)
    norm0 = jnp.zeros((NX, NY), jnp.float32)

    def per_device(index, carry):
        dev_w = index // N_NARROW
        dev_n = index % N_NARROW
        feats = features[dev_w, dev_n]
        ids = patch_ids[dev_w, dev_n]
        count = patch_count[dev_w, dev_n]
        weighted = patch_head(feats, mlp_weight, mlp_bias, out_weight, out_bias, gauss)

        def per_patch(slot, inner):
            total, norm = inner
            live = (slot < count).astype(jnp.float32)
            start_x = ((ids[slot] // rows_q) * quad).astype(jnp.int32)
            start_y = ((ids[slot] % rows_q) * quad).astype(jnp.int32)
            zero = jnp.zeros((), jnp.int32)
            block = weighted[slot].astype(jnp.float32).reshape(CLASSES, PATCH, PATCH) * live
            old = lax.dynamic_slice(total, (zero, start_x, start_y), (CLASSES, PATCH, PATCH))
            total = lax.dynamic_update_slice(total, old + block, (zero, start_x, start_y))
            old_norm = lax.dynamic_slice(norm, (start_x, start_y), (PATCH, PATCH))
            norm = lax.dynamic_update_slice(norm, old_norm + gauss_square * live, (start_x, start_y))
            return total, norm

        return lax.fori_loop(0, PSLOT, per_patch, carry)

    total, norm = lax.fori_loop(0, N_WIDE * N_NARROW, per_device, (total0, norm0))
    background = (jnp.arange(CLASSES) == 0).astype(jnp.float32)[:, None, None]
    blended = ((total + 0.001 * background) / (norm + 0.001)[None]).astype(jnp.bfloat16)

    def per_class(item):
        plane, klass = item
        prob = plane.astype(jnp.float32)
        truth = (labels == klass).astype(jnp.float32)
        prob_edge = edge_of(prob)
        truth_edge = edge_of(truth)
        prob_wide = spread_of(prob_edge)
        truth_wide = spread_of(truth_edge)
        numer_map = prob_edge * truth_wide + truth_edge * prob_wide
        denom_map = prob_edge + truth_edge
        whole = jnp.stack([jnp.sum(numer_map), jnp.sum(denom_map)])
        slabs = jnp.stack([slab_total(numer_map), slab_total(denom_map)])
        return whole, slabs

    sums, slabs = lax.map(per_class, (blended, jnp.arange(CLASSES, dtype=jnp.int32)))
    dice = (sums[:, 0] + 1.0) / (sums[:, 1] + 1.0)
    slab_sums = slabs.transpose(2, 3, 1, 0) / jnp.float32(SX)
    return blended, dice, slab_sums
```

```python
import functools

import jax
import jax.numpy as jnp
from jax import lax
from jax.experimental import pallas as pl
from jax.experimental.pallas import tpu as pltpu
from jax.sharding import PartitionSpec as P

PATCH = 96
QUAD = 48
TILE = 128
RING = 256
ROWS = 4
CHUNKS = ((0, 16), (16, 16), (32, 16))
VMEM_LIMIT = 50 * 1024 * 1024


def pack_kernel(first, rows, pick_ref, feats_ref, out_ref, sems):
    width = rows * PATCH

    def copy_of(column):
        source = jnp.maximum(pick_ref[column], 0)
        start = first if column % 2 == 0 else QUAD - first - rows
        lane = pl.multiple_of((source % 2) * (QUAD * PATCH) + start * PATCH, TILE)
        return pltpu.make_async_copy(
            feats_ref.at[source // 2, :, pl.ds(lane, width)], out_ref.at[column], sems.at[column]
        )

    columns = out_ref.shape[0]
    for column in range(columns):
        copy_of(column).start()
    for column in range(columns):
        copy_of(column).wait()


def pack(feats, pick, first, rows):
    columns = pick.shape[0]
    width = rows * PATCH
    return pl.pallas_call(
        functools.partial(pack_kernel, first, rows),
        out_shape=jax.ShapeDtypeStruct((columns, feats.shape[1], width), feats.dtype),
        in_specs=[pl.BlockSpec(memory_space=pltpu.SMEM), pl.BlockSpec(memory_space=pl.ANY)],
        out_specs=pl.BlockSpec(memory_space=pl.ANY),
        scratch_shapes=[pltpu.SemaphoreType.DMA((columns,))],
        cost_estimate=pl.CostEstimate(
            flops=0, bytes_accessed=columns * width * feats.shape[1] * 4, transcendentals=0
        ),
        name="pack",
    )(pick, feats)


def spread_rows(tiles, lane):
    one, two, three = tiles
    return (
        one,
        jnp.where(lane < 32, pltpu.roll(one, 32, 1), pltpu.roll(two, 32, 1)),
        jnp.where(lane < 64, pltpu.roll(two, 64, 1), pltpu.roll(three, 64, 1)),
        pltpu.roll(three, 96, 1),
    )


def head_kernel(
    first, rows, classes, code_ref, recv_ref, mlp_ref, bias_ref, head_ref, gauss_ref,
    own_ref, up_ref, down_ref, acc_ref, edge_ref,
):
    feat = recv_ref.shape[1]
    padded = head_ref.shape[0]
    lane_feat = lax.broadcasted_iota(jnp.int32, (feat, TILE), 1)
    lane = lax.broadcasted_iota(jnp.int32, (padded, TILE), 1)
    real = lax.broadcasted_iota(jnp.int32, (padded, TILE), 0) < classes
    mlp = mlp_ref[...]
    head = head_ref[...]
    extra = jnp.ones((head.shape[1] - feat, 4 * TILE), jnp.bfloat16)

    @pl.loop(0, ROWS)
    def _(which):
        @pl.loop(0, 2 * rows)
        def _(row):
            acc_ref[which, row] = jnp.zeros((padded, TILE), jnp.float32)

    edge_ref[...] = jnp.zeros_like(edge_ref)

    @pl.loop(0, code_ref[2 * 16])
    def _(item):
        code = code_ref[item]
        slot = code // 8
        which = (code // 2) % 4
        side = slot % 2
        start = (code % 2) * QUAD + jnp.where(side == 0, first, QUAD - first - rows)
        for group in range(rows // 4):
            at = group * 3 * TILE
            tiles = [
                recv_ref[slot, :, at + i * TILE : at + (i + 1) * TILE].astype(jnp.float32)
                for i in range(3)
            ]
            voxels = jnp.concatenate(spread_rows(tiles, lane_feat), axis=1)
            hidden = jnp.dot(
                mlp, voxels.astype(jnp.bfloat16), preferred_element_type=jnp.float32
            )
            bias = jnp.concatenate([bias_ref[...]] * 4, axis=1)
            active = (voxels + jnp.maximum(hidden + bias, 0.0)).astype(jnp.bfloat16)
            logits = jnp.dot(
                head, jnp.concatenate([active, extra], axis=0), preferred_element_type=jnp.float32
            )
            for i in range(4):
                part = logits[:, i * TILE : (i + 1) * TILE]
                top = jnp.max(part, axis=0, keepdims=True)
                raised = jnp.where(real, jnp.exp(part - top), 0.0)
                scale = gauss_ref[pl.ds(start + group * 4 + i, 1), :] / jnp.sum(
                    raised, axis=0, keepdims=True
                )
                row = side * rows + group * 4 + i
                acc_ref[which, row] += (
                    (raised * scale).astype(jnp.bfloat16).astype(jnp.float32)
                )

    def merged(row):
        a0, a1, a2, a3 = [acc_ref[which, row] for which in range(ROWS)]
        a1 = pltpu.roll(a1, 48, 1)
        a2 = pltpu.roll(a2, 96, 1)
        low = a0 + jnp.where(lane >= 48, a1, 0.0) + jnp.where(lane >= 96, a2, 0.0)
        high = (
            jnp.where(lane < 48, a1, 0.0)
            + jnp.where(lane < 96, a2, 0.0)
            + pltpu.roll(a3, 16, 1)
        )
        own_ref[row, :, 0:TILE] = low
        own_ref[row, :, TILE:RING] = high
        edge_ref[...] = jnp.where(
            (lane == 2 * row) | (lane == 2 * row + 1), pltpu.roll(low, 2 * row, 1), edge_ref[...]
        )
        return high

    @pl.loop(0, rows)
    def _(pair):
        even = merged(2 * pair)
        odd = merged(2 * pair + 1)
        up_ref[pair] = jnp.where(lane < 64, pltpu.roll(even, 66, 1), pltpu.roll(odd, 2, 1)).astype(
            jnp.bfloat16
        )

    down_ref[...] = edge_ref[...].astype(jnp.bfloat16)


def head_of(recv, codes, mlp_weight, bias_tile, head_weight, gauss, first, rows, classes):
    padded = head_weight.shape[0]
    whole = pl.BlockSpec(memory_space=pltpu.VMEM)
    return pl.pallas_call(
        functools.partial(head_kernel, first, rows, classes),
        out_shape=(
            jax.ShapeDtypeStruct((2 * rows, padded, RING), jnp.float32),
            jax.ShapeDtypeStruct((rows, padded, TILE), jnp.bfloat16),
            jax.ShapeDtypeStruct((padded, TILE), jnp.bfloat16),
        ),
        in_specs=[pl.BlockSpec(memory_space=pltpu.SMEM)] + [whole] * 5,
        out_specs=(whole, whole, whole),
        scratch_shapes=[
            pltpu.VMEM((ROWS, 2 * rows, padded, TILE), jnp.float32),
            pltpu.VMEM((padded, TILE), jnp.float32),
        ],
        compiler_params=pltpu.CompilerParams(vmem_limit_bytes=VMEM_LIMIT),
        cost_estimate=pl.CostEstimate(
            flops=rows * 900_000_000 // 48, bytes_accessed=rows * 25_000_000 // 48,
            transcendentals=rows * 12_000_000 // 48,
        ),
        name="head",
    )(codes, recv, mlp_weight, bias_tile, head_weight, gauss)


def blend_kernel(own_ref, up_ref, down_ref, inv_ref, prob_ref):
    rows, padded, _ = own_ref.shape
    lane = lax.broadcasted_iota(jnp.int32, (padded, TILE), 1)
    first = lax.broadcasted_iota(jnp.int32, (padded, TILE), 0) == 0
    extra = jnp.where(first, 0.001, 0.0)
    down = down_ref[...].astype(jnp.float32)

    def one(row, came, shift):
        came = pltpu.roll(came, shift, 1)
        low = own_ref[row, :, 0:TILE] + jnp.where(lane < 48, came, 0.0)
        high = own_ref[row, :, TILE:RING] + jnp.where(lane >= 126, came, 0.0)
        after = pltpu.roll(down, lax.rem(192 - 2 * row, TILE), 1)
        high = high + jnp.where((lane == 64) | (lane == 65), after, 0.0)
        scale = inv_ref[pl.ds(row, 1), :]
        prob_ref[row, :, 0:TILE] = ((low + extra) * scale[:, 0:TILE]).astype(jnp.bfloat16)
        prob_ref[row, :, TILE:RING] = ((high + extra) * scale[:, TILE:RING]).astype(jnp.bfloat16)

    @pl.loop(0, rows // 2)
    def _(pair):
        came = up_ref[pair].astype(jnp.float32)
        one(2 * pair, came, 126)
        one(2 * pair + 1, came, 62)


def blend_of(own, up, down, inv):
    whole = pl.BlockSpec(memory_space=pltpu.VMEM)
    return pl.pallas_call(
        blend_kernel,
        out_shape=jax.ShapeDtypeStruct(own.shape, jnp.bfloat16),
        in_specs=[whole] * 4,
        out_specs=whole,
        compiler_params=pltpu.CompilerParams(vmem_limit_bytes=VMEM_LIMIT),
        cost_estimate=pl.CostEstimate(
            flops=own.size * 4, bytes_accessed=own.size * 7, transcendentals=0
        ),
        name="blend",
    )(own, up, down, inv)


def turn(tiles, forward, lane):
    low, high = tiles
    shift, at = (1, 0) if forward else (TILE - 1, TILE - 1)
    low, high = pltpu.roll(low, shift, 1), pltpu.roll(high, shift, 1)
    return jnp.where(lane == at, high, low), jnp.where(lane == at, low, high)


def dice_kernel(prob_ref, label_ref, sums_ref, edge_ref, numer_ref, denom_ref):
    padded = prob_ref.shape[1]
    rows = prob_ref.shape[0] - 4
    lane = lax.broadcasted_iota(jnp.int32, (8, TILE), 1)
    klass = lax.broadcasted_iota(jnp.int32, (8, TILE), 0) + 1
    owned = (lane < TILE, lane < 64)

    def tiles_of(ref, row, group):
        return [
            ref[row, group : group + 8, i * TILE : (i + 1) * TILE].astype(jnp.float32)
            for i in range(2)
        ]

    @pl.loop(0, rows + 2)
    def _(row):
        for group in range(0, padded, 8):
            centre = tiles_of(prob_ref, row + 1, group)
            before, after = tiles_of(prob_ref, row, group), tiles_of(prob_ref, row + 2, group)
            left, right = turn(centre, True, lane), turn(centre, False, lane)
            for i in range(2):
                low = jnp.minimum(
                    jnp.minimum(before[i], after[i]), jnp.minimum(left[i], right[i])
                )
                edge_ref[row, group : group + 8, i * TILE : (i + 1) * TILE] = centre[
                    i
                ] - jnp.minimum(centre[i], low)

    numer_ref[...] = jnp.zeros_like(numer_ref)
    denom_ref[...] = jnp.zeros_like(denom_ref)

    @pl.loop(0, rows)
    def _(row):
        def labels_of(at):
            line = label_ref[pl.ds(at, 1), :]
            return [
                jnp.broadcast_to(line[:, i * TILE : (i + 1) * TILE], (8, TILE)) for i in range(2)
            ]

        middle = labels_of(row + 1)
        near = (labels_of(row), labels_of(row + 2), turn(middle, True, lane), turn(middle, False, lane))
        for group in range(0, padded, 8):
            centre = tiles_of(edge_ref, row + 1, group)
            before, after = tiles_of(edge_ref, row, group), tiles_of(edge_ref, row + 2, group)
            left, right = turn(centre, True, lane), turn(centre, False, lane)
            numer = numer_ref[group : group + 8, :]
            denom = denom_ref[group : group + 8, :]
            for i in range(2):
                wide = jnp.maximum(
                    jnp.maximum(centre[i], jnp.maximum(before[i], after[i])),
                    jnp.maximum(left[i], right[i]),
                )
                here = middle[i] == klass + group
                about = here
                for other in near:
                    about = about | (other[i] == klass + group)
                value = jnp.where(about, centre[i], 0.0) + jnp.where(here, wide, 0.0)
                total = centre[i] + jnp.where(here, 1.0, 0.0)
                if i == 1:
                    value = jnp.where(owned[i], value, 0.0)
                    total = jnp.where(owned[i], total, 0.0)
                numer = numer + value
                denom = denom + total
            numer_ref[group : group + 8, :] = numer
            denom_ref[group : group + 8, :] = denom

    sums_ref[0] = jnp.broadcast_to(
        jnp.sum(numer_ref[...], axis=1, keepdims=True), (padded, TILE)
    )
    sums_ref[1] = jnp.broadcast_to(
        jnp.sum(denom_ref[...], axis=1, keepdims=True), (padded, TILE)
    )


def dice_of(prob, label):
    rows, padded, _ = prob.shape
    whole = pl.BlockSpec(memory_space=pltpu.VMEM)
    return pl.pallas_call(
        dice_kernel,
        out_shape=jax.ShapeDtypeStruct((2, padded, TILE), jnp.float32),
        in_specs=[whole] * 2,
        out_specs=whole,
        scratch_shapes=[
            pltpu.VMEM((rows - 2, padded, RING), jnp.float32),
            pltpu.VMEM((padded, TILE), jnp.float32),
            pltpu.VMEM((padded, TILE), jnp.float32),
        ],
        compiler_params=pltpu.CompilerParams(vmem_limit_bytes=VMEM_LIMIT),
        cost_estimate=pl.CostEstimate(
            flops=prob.size * 30, bytes_accessed=prob.size * 2, transcendentals=0
        ),
        name="dice",
    )(prob, label)


def shifted(block, axis, by):
    devices = lax.axis_size(axis)
    pairs = [(i, i + by) for i in range(devices) if 0 <= i + by < devices]
    return lax.ppermute(block, axis, pairs)


def padded_2(block, sides, width):
    for axis, dim in sides:
        low = shifted(lax.slice_in_dim(block, block.shape[dim] - width, None, axis=dim), axis, 1)
        high = shifted(lax.slice_in_dim(block, 0, width, axis=dim), axis, -1)
        block = jnp.concatenate([low, block, high], axis=dim)
    return block


def gauss_line():
    position = jnp.arange(PATCH, dtype=jnp.float32) - (PATCH - 1) / 2.0
    sigma = 0.125 * PATCH
    return position * position / (2.0 * sigma * sigma)


def gauss_table():
    line = gauss_line()
    table = jnp.exp(-(line[:, None] + line[None, :]))
    return jnp.pad(table, ((0, 0), (0, TILE - PATCH)))


def three_parts(values):
    high = values.astype(jnp.bfloat16)
    rest = values - high.astype(jnp.float32)
    middle = rest.astype(jnp.bfloat16)
    low = (rest - middle.astype(jnp.float32)).astype(jnp.bfloat16)
    return jnp.stack([high, middle, low], axis=1)


def head_matrix(out_weight, out_bias):
    classes, feat = out_weight.shape
    matrix = jnp.concatenate(
        [out_weight, three_parts(out_bias), jnp.zeros((classes, 13), jnp.bfloat16)], axis=1
    )
    return jnp.concatenate([matrix, matrix[-2:]], axis=0)


def ring_of(plane):
    gap = jnp.zeros((plane.shape[0], RING - plane.shape[1]), plane.dtype)
    return jnp.concatenate([plane[:, 2:], gap, plane[:, :2]], axis=1)


def rows_of(plane, first, rows):
    span = plane.shape[0]
    return jnp.concatenate(
        [plane[first : first + rows], plane[span - first - rows : span - first]], axis=0
    )


def on_device(features, patch_ids, patch_count, labels, mlp_weight, mlp_bias, out_weight, out_bias):
    wide, narrow = lax.axis_size("wide"), lax.axis_size("narrow")
    here_wide, here_narrow = lax.axis_index("wide"), lax.axis_index("narrow")
    feat = features.shape[3]
    slots = features.shape[2]
    classes = out_weight.shape[0]
    span_x, span_y = labels.shape
    rows_q = ROWS * narrow
    feats = features[0, 0]

    slot_ids = jnp.arange(slots, dtype=jnp.int32)
    halves = jnp.arange(2, dtype=jnp.int32)
    columns = jnp.arange(2 * wide, dtype=jnp.int32)
    listed = slot_ids < patch_count[0, 0]
    column_of = patch_ids[0, 0][:, None] // rows_q + halves[None, :]
    hit = listed[:, None, None] & (column_of[:, :, None] == columns[None, None, :])
    pick = jnp.max(
        jnp.where(hit, (2 * slot_ids[:, None] + halves[None, :])[:, :, None], -1), axis=(0, 1)
    )

    payloads = [pack(feats, pick, first, rows) for first, rows in CHUNKS]
    received = [
        lax.all_to_all(
            payload.reshape(wide, 2, feat, payload.shape[2]), "wide", 0, 0, tiled=True
        ).reshape(2 * wide, feat, payload.shape[2])
        for payload in payloads
    ]

    listing = jnp.concatenate([patch_ids[0, 0], patch_count[0]])
    listing = lax.all_gather(listing, "wide")
    all_ids, all_count = listing[:, :slots], listing[:, slots]
    all_listed = slot_ids[None, :] < all_count[:, None]
    mine = 2 * here_wide + halves
    all_column = (all_ids // rows_q)[:, :, None] + halves[None, None, :]
    match = all_listed[:, :, None, None] & (all_column[:, :, :, None] == mine)
    kind = (all_ids % rows_q - ROWS * here_narrow)[:, :, None] * 2 + halves[None, None, :]
    tag = jnp.max(jnp.where(match, kind[:, :, :, None], -1), axis=(1, 2)).reshape(-1)
    valid = tag >= 0
    order = jnp.cumsum(valid.astype(jnp.int32)) - 1
    code = jnp.where(valid, columns * 8 + tag, 0)
    place = valid[:, None] & (order[:, None] == columns[None, :])
    codes = jnp.concatenate(
        [
            jnp.sum(jnp.where(place, code[:, None], 0), axis=0),
            jnp.sum(valid.astype(jnp.int32))[None],
        ]
    )

    table = gauss_table()
    line = table[:, :PATCH]
    kinds = jnp.arange(2 * ROWS, dtype=jnp.int32)
    counts = jnp.sum(
        (tag.reshape(wide, 2, 1) == kinds).astype(jnp.float32), axis=0
    ).reshape(2, ROWS, 2)
    square = line.reshape(2, QUAD, PATCH)
    by_row = jnp.sum(
        counts[:, :, :, None, None] * square[None, None], axis=2
    )
    by_row = by_row.transpose(1, 0, 2, 3).reshape(ROWS, span_x, PATCH)
    norm = sum(
        jnp.pad(by_row[i], ((0, 0), (QUAD * i, QUAD * (ROWS - 1 - i)))) for i in range(ROWS)
    )
    came_low = shifted(norm[:, span_y - 2 :], "narrow", 1)
    came_high = shifted(norm[:, :2], "narrow", -1)
    norm = jnp.concatenate(
        [
            came_low[:, :2],
            norm[:, :QUAD] + came_low[:, 2:],
            norm[:, QUAD:span_y],
            norm[:, span_y : span_y + 2] + came_high,
        ],
        axis=1,
    )
    across = ROWS * QUAD * here_narrow - 2 + jnp.arange(span_y + 4, dtype=jnp.int32)
    inside = (across >= 0) & (across < narrow * span_y)
    inverse = ring_of(jnp.where(inside[None, :], 1.0 / (norm + 0.001), 0.0))

    label_wide = padded_2(labels + 1, (("wide", 0), ("narrow", 1)), 2)
    centre = label_wide[1:-1, 1:-1]
    same = (
        (label_wide[:-2, 1:-1] == centre)
        & (label_wide[2:, 1:-1] == centre)
        & (label_wide[1:-1, :-2] == centre)
        & (label_wide[1:-1, 2:] == centre)
    )
    boundary = jnp.where(same, 0, centre)
    boundary = ring_of(jnp.pad(boundary, ((0, 0), (1, 1))))

    head_weight = head_matrix(out_weight, out_bias)
    bias_tile = jnp.broadcast_to(mlp_bias[:, None], (feat, TILE))
    probs = []
    for (first, rows), recv in zip(CHUNKS, received):
        own, up, down = head_of(
            recv, codes, mlp_weight, bias_tile, head_weight, table, first, rows, classes
        )
        up = shifted(up, "narrow", 1)
        down = shifted(down, "narrow", -1)
        probs.append(blend_of(own, up, down, rows_of(inverse, first, rows)))
    edge_rows = CHUNKS[0][1]
    before = shifted(probs[0][2 * edge_rows - 2 :], "wide", 1)
    after = shifted(probs[0][:2], "wide", -1)
    pieces = [prob[:rows] for prob, (_, rows) in zip(probs, CHUNKS)]
    pieces += [prob[rows:] for prob, (_, rows) in zip(probs[::-1], CHUNKS[::-1])]
    prob = jnp.concatenate([before] + pieces + [after], axis=0)
    blended = prob[2:-2, :classes, :span_y].transpose(1, 0, 2)
    sums = dice_of(prob, boundary)[:, :classes, 0]
    slab_sums = (sums / jnp.float32(span_x)).reshape(1, 1, 2, classes)
    whole = lax.psum(sums, ("wide", "narrow"))
    dice = (whole[0] + 1.0) / (whole[1] + 1.0)
    return (blended, dice, slab_sums)


def solution(mesh):
    return jax.shard_map(
        on_device,
        mesh=mesh,
        in_specs=(
            P("wide", "narrow", None, None, None),
            P("wide", "narrow", None),
            P("wide", "narrow"),
            P("wide", "narrow"),
            P(),
            P(),
            P(),
            P(),
        ),
        out_specs=(P(None, "wide", "narrow"), P(), P("wide", "narrow", None, None)),
        check_vma=False,
    )
```

```python
import functools

import jax
import jax.numpy as jnp
from jax import lax
from jax.experimental import pallas as pl
from jax.experimental.pallas import tpu as pltpu
from jax.sharding import PartitionSpec as P

PATCH = 96
QUAD = 48
TILE = 128
RING = 256
ROWS = 4
CHUNKS = ((0, 16), (16, 16), (32, 16))
VMEM_LIMIT = 50 * 1024 * 1024


def pack_kernel(first, rows, pick_ref, feats_ref, out_ref, sems):
    width = rows * PATCH

    def copy_of(column):
        source = pick_ref[column]
        start = first if column % 2 == 0 else QUAD - first - rows
        lane = pl.multiple_of((source % 2) * (QUAD * PATCH) + start * PATCH, TILE)
        return pltpu.make_async_copy(
            feats_ref.at[source // 2, :, pl.ds(lane, width)], out_ref.at[column], sems.at[column]
        )

    columns = out_ref.shape[0]
    for column in range(columns):

        @pl.when(pick_ref[column] >= 0)
        def _():
            copy_of(column).start()

    for column in range(columns):

        @pl.when(pick_ref[column] >= 0)
        def _():
            copy_of(column).wait()


def pack(feats, pick, first, rows):
    columns = pick.shape[0]
    width = rows * PATCH
    return pl.pallas_call(
        functools.partial(pack_kernel, first, rows),
        out_shape=jax.ShapeDtypeStruct((columns, feats.shape[1], width), feats.dtype),
        in_specs=[pl.BlockSpec(memory_space=pltpu.SMEM), pl.BlockSpec(memory_space=pl.ANY)],
        out_specs=pl.BlockSpec(memory_space=pltpu.VMEM),
        scratch_shapes=[pltpu.SemaphoreType.DMA((columns,))],
        compiler_params=pltpu.CompilerParams(vmem_limit_bytes=VMEM_LIMIT),
        cost_estimate=pl.CostEstimate(
            flops=0, bytes_accessed=columns * width * feats.shape[1] * 4, transcendentals=0
        ),
        name="pack",
    )(pick, feats)


def spread_rows(tiles, lane):
    one, two, three = tiles
    return (
        one,
        jnp.where(lane < 32, pltpu.roll(one, 32, 1), pltpu.roll(two, 32, 1)),
        jnp.where(lane < 64, pltpu.roll(two, 64, 1), pltpu.roll(three, 64, 1)),
        pltpu.roll(three, 96, 1),
    )


def head_kernel(
    first, rows, classes, code_ref, recv_ref, mlp_ref, bias_ref, head_ref, gauss_ref,
    own_ref, up_ref, down_ref, acc_ref, edge_ref, act_ref,
):
    feat = recv_ref.shape[1]
    padded = head_ref.shape[0]
    lane_feat = lax.broadcasted_iota(jnp.int32, (feat, TILE), 1)
    lane = lax.broadcasted_iota(jnp.int32, (padded, TILE), 1)
    real = lax.broadcasted_iota(jnp.int32, (padded, TILE), 0) < classes
    mlp = mlp_ref[...]
    head = head_ref[...]
    act_ref[feat:, :] = jnp.ones((act_ref.shape[0] - feat, act_ref.shape[1]), jnp.bfloat16)

    @pl.loop(0, ROWS)
    def _(which):
        @pl.loop(0, 2 * rows)
        def _(row):
            acc_ref[which, row] = jnp.zeros((padded, TILE), jnp.float32)

    edge_ref[...] = jnp.zeros_like(edge_ref)

    @pl.loop(0, code_ref[2 * 16])
    def _(item):
        code = code_ref[item]
        slot = code // 8
        which = (code // 2) % 4
        side = slot % 2
        start = (code % 2) * QUAD + jnp.where(side == 0, first, QUAD - first - rows)
        flat = recv_ref[slot]
        hidden = jnp.dot(mlp, flat, preferred_element_type=jnp.float32)
        for group in range(rows // 4):
            tiles = []
            for i in range(3):
                part = slice((group * 3 + i) * TILE, (group * 3 + i + 1) * TILE)
                tiles.append(
                    flat[:, part].astype(jnp.float32)
                    + jnp.maximum(hidden[:, part] + bias_ref[...], 0.0)
                )
            for i, tile in enumerate(spread_rows(tiles, lane_feat)):
                at = (group * 4 + i) * TILE
                act_ref[0:feat, at : at + TILE] = tile.astype(jnp.bfloat16)
        logits = jnp.dot(head, act_ref[...], preferred_element_type=jnp.float32)
        for i in range(rows):
            part = logits[:, i * TILE : (i + 1) * TILE]
            top = jnp.max(part, axis=0, keepdims=True)
            raised = jnp.where(real, jnp.exp(part - top), 0.0)
            scale = gauss_ref[pl.ds(start + i, 1), :] / jnp.sum(raised, axis=0, keepdims=True)
            acc_ref[which, side * rows + i] += (
                (raised * scale).astype(jnp.bfloat16).astype(jnp.float32)
            )

    def merged(row):
        a0, a1, a2, a3 = [acc_ref[which, row] for which in range(ROWS)]
        a1 = pltpu.roll(a1, 48, 1)
        a2 = pltpu.roll(a2, 96, 1)
        low = a0 + jnp.where(lane >= 48, a1, 0.0) + jnp.where(lane >= 96, a2, 0.0)
        high = (
            jnp.where(lane < 48, a1, 0.0)
            + jnp.where(lane < 96, a2, 0.0)
            + pltpu.roll(a3, 16, 1)
        )
        own_ref[row, :, 0:TILE] = low
        own_ref[row, :, TILE:RING] = high
        edge_ref[...] = jnp.where(
            (lane == 2 * row) | (lane == 2 * row + 1), pltpu.roll(low, 2 * row, 1), edge_ref[...]
        )
        return high

    @pl.loop(0, rows)
    def _(pair):
        even = merged(2 * pair)
        odd = merged(2 * pair + 1)
        up_ref[pair] = jnp.where(lane < 64, pltpu.roll(even, 66, 1), pltpu.roll(odd, 2, 1)).astype(
            jnp.bfloat16
        )

    down_ref[...] = edge_ref[...].astype(jnp.bfloat16)


def head_of(recv, codes, mlp_weight, bias_tile, head_weight, gauss, first, rows, classes):
    padded = head_weight.shape[0]
    whole = pl.BlockSpec(memory_space=pltpu.VMEM)
    return pl.pallas_call(
        functools.partial(head_kernel, first, rows, classes),
        out_shape=(
            jax.ShapeDtypeStruct((2 * rows, padded, RING), jnp.float32),
            jax.ShapeDtypeStruct((rows, padded, TILE), jnp.bfloat16),
            jax.ShapeDtypeStruct((padded, TILE), jnp.bfloat16),
        ),
        in_specs=[pl.BlockSpec(memory_space=pltpu.SMEM)] + [whole] * 5,
        out_specs=(whole, whole, whole),
        scratch_shapes=[
            pltpu.VMEM((ROWS, 2 * rows, padded, TILE), jnp.float32),
            pltpu.VMEM((padded, TILE), jnp.float32),
            pltpu.VMEM((head_weight.shape[1], rows * TILE), jnp.bfloat16),
        ],
        compiler_params=pltpu.CompilerParams(vmem_limit_bytes=VMEM_LIMIT),
        cost_estimate=pl.CostEstimate(
            flops=rows * 900_000_000 // 48, bytes_accessed=rows * 25_000_000 // 48,
            transcendentals=rows * 12_000_000 // 48,
        ),
        name="head",
    )(codes, recv, mlp_weight, bias_tile, head_weight, gauss)


def blend_kernel(own_ref, up_ref, down_ref, inv_ref, prob_ref):
    rows, padded, _ = own_ref.shape
    lane = lax.broadcasted_iota(jnp.int32, (padded, TILE), 1)
    first = lax.broadcasted_iota(jnp.int32, (padded, TILE), 0) == 0
    extra = jnp.where(first, 0.001, 0.0)
    down = down_ref[...].astype(jnp.float32)

    def one(row, came, shift):
        came = pltpu.roll(came, shift, 1)
        low = own_ref[row, :, 0:TILE] + jnp.where(lane < 48, came, 0.0)
        high = own_ref[row, :, TILE:RING] + jnp.where(lane >= 126, came, 0.0)
        after = pltpu.roll(down, lax.rem(192 - 2 * row, TILE), 1)
        high = high + jnp.where((lane == 64) | (lane == 65), after, 0.0)
        scale = inv_ref[pl.ds(row, 1), :]
        prob_ref[row, :, 0:TILE] = ((low + extra) * scale[:, 0:TILE]).astype(jnp.bfloat16)
        prob_ref[row, :, TILE:RING] = ((high + extra) * scale[:, TILE:RING]).astype(jnp.bfloat16)

    @pl.loop(0, rows // 2)
    def _(pair):
        came = up_ref[pair].astype(jnp.float32)
        one(2 * pair, came, 126)
        one(2 * pair + 1, came, 62)


def blend_of(own, up, down, inv):
    whole = pl.BlockSpec(memory_space=pltpu.VMEM)
    return pl.pallas_call(
        blend_kernel,
        out_shape=jax.ShapeDtypeStruct(own.shape, jnp.bfloat16),
        in_specs=[whole] * 4,
        out_specs=whole,
        compiler_params=pltpu.CompilerParams(vmem_limit_bytes=VMEM_LIMIT),
        cost_estimate=pl.CostEstimate(
            flops=own.size * 4, bytes_accessed=own.size * 7, transcendentals=0
        ),
        name="blend",
    )(own, up, down, inv)


def turn(tiles, forward, lane):
    low, high = tiles
    shift, at = (1, 0) if forward else (TILE - 1, TILE - 1)
    low, high = pltpu.roll(low, shift, 1), pltpu.roll(high, shift, 1)
    return jnp.where(lane == at, high, low), jnp.where(lane == at, low, high)


def dice_kernel(prob_ref, label_ref, sums_ref, edge_ref, numer_ref, denom_ref):
    padded = prob_ref.shape[1]
    rows = prob_ref.shape[0] - 4
    lane = lax.broadcasted_iota(jnp.int32, (8, TILE), 1)
    klass = lax.broadcasted_iota(jnp.int32, (8, TILE), 0) + 1
    owned = (lane < TILE, lane < 64)

    def tiles_of(ref, row, group):
        return [
            ref[row, group : group + 8, i * TILE : (i + 1) * TILE].astype(jnp.float32)
            for i in range(2)
        ]

    @pl.loop(0, rows + 2)
    def _(row):
        for group in range(0, padded, 8):
            centre = tiles_of(prob_ref, row + 1, group)
            before, after = tiles_of(prob_ref, row, group), tiles_of(prob_ref, row + 2, group)
            left, right = turn(centre, True, lane), turn(centre, False, lane)
            for i in range(2):
                low = jnp.minimum(
                    jnp.minimum(before[i], after[i]), jnp.minimum(left[i], right[i])
                )
                edge_ref[row, group : group + 8, i * TILE : (i + 1) * TILE] = centre[
                    i
                ] - jnp.minimum(centre[i], low)

    numer_ref[...] = jnp.zeros_like(numer_ref)
    denom_ref[...] = jnp.zeros_like(denom_ref)

    @pl.loop(0, rows)
    def _(row):
        def labels_of(at):
            line = label_ref[pl.ds(at, 1), :]
            return [
                jnp.broadcast_to(line[:, i * TILE : (i + 1) * TILE], (8, TILE)) for i in range(2)
            ]

        middle = labels_of(row + 1)
        near = (labels_of(row), labels_of(row + 2), turn(middle, True, lane), turn(middle, False, lane))
        for group in range(0, padded, 8):
            centre = tiles_of(edge_ref, row + 1, group)
            before, after = tiles_of(edge_ref, row, group), tiles_of(edge_ref, row + 2, group)
            left, right = turn(centre, True, lane), turn(centre, False, lane)
            numer = numer_ref[group : group + 8, :]
            denom = denom_ref[group : group + 8, :]
            for i in range(2):
                wide = jnp.maximum(
                    jnp.maximum(centre[i], jnp.maximum(before[i], after[i])),
                    jnp.maximum(left[i], right[i]),
                )
                here = middle[i] == klass + group
                about = here
                for other in near:
                    about = about | (other[i] == klass + group)
                value = jnp.where(about, centre[i], 0.0) + jnp.where(here, wide, 0.0)
                total = centre[i] + jnp.where(here, 1.0, 0.0)
                if i == 1:
                    value = jnp.where(owned[i], value, 0.0)
                    total = jnp.where(owned[i], total, 0.0)
                numer = numer + value
                denom = denom + total
            numer_ref[group : group + 8, :] = numer
            denom_ref[group : group + 8, :] = denom

    sums_ref[0] = jnp.broadcast_to(
        jnp.sum(numer_ref[...], axis=1, keepdims=True), (padded, TILE)
    )
    sums_ref[1] = jnp.broadcast_to(
        jnp.sum(denom_ref[...], axis=1, keepdims=True), (padded, TILE)
    )


def dice_of(prob, label):
    rows, padded, _ = prob.shape
    whole = pl.BlockSpec(memory_space=pltpu.VMEM)
    return pl.pallas_call(
        dice_kernel,
        out_shape=jax.ShapeDtypeStruct((2, padded, TILE), jnp.float32),
        in_specs=[whole] * 2,
        out_specs=whole,
        scratch_shapes=[
            pltpu.VMEM((rows - 2, padded, RING), jnp.float32),
            pltpu.VMEM((padded, TILE), jnp.float32),
            pltpu.VMEM((padded, TILE), jnp.float32),
        ],
        compiler_params=pltpu.CompilerParams(vmem_limit_bytes=VMEM_LIMIT),
        cost_estimate=pl.CostEstimate(
            flops=prob.size * 30, bytes_accessed=prob.size * 2, transcendentals=0
        ),
        name="dice",
    )(prob, label)


def emit_kernel(low, high, prob_ref, *refs):
    out_ref, turned_ref, sems = refs[-3:]
    rows, padded, _ = prob_ref.shape
    classes, _, span_y = out_ref.shape
    half = rows // 2

    @pl.loop(0, padded // 8)
    def _(index):
        group = pl.multiple_of(index * 8, 8)
        for at in range(0, rows, 8):
            for i in range(2):
                lanes = slice(i * TILE, min((i + 1) * TILE, span_y))
                block = prob_ref[at : at + 8, pl.ds(group, 8), i * TILE : (i + 1) * TILE]
                block = jnp.transpose(block.astype(jnp.float32), (1, 0, 2))
                turned_ref[pl.ds(group, 8), at : at + 8, lanes] = block[
                    :, :, : lanes.stop - lanes.start
                ].astype(jnp.bfloat16)

    copies = [
        pltpu.make_async_copy(
            turned_ref.at[pl.ds(0, classes), pl.ds(i * half, half), :],
            out_ref.at[:, pl.ds(at, half), :],
            sems.at[i],
        )
        for i, at in enumerate((low, high))
    ]
    for copy in copies:
        copy.start()
    for copy in copies:
        copy.wait()


def emit(prob, low, high, shape, out=None):
    rows, padded, _ = prob.shape
    anywhere = pl.BlockSpec(memory_space=pl.ANY)
    before = () if out is None else (out,)
    return pl.pallas_call(
        functools.partial(emit_kernel, low, high),
        out_shape=jax.ShapeDtypeStruct(shape, prob.dtype),
        in_specs=[pl.BlockSpec(memory_space=pltpu.VMEM)] + [anywhere] * len(before),
        out_specs=anywhere,
        input_output_aliases={1: 0} if before else {},
        scratch_shapes=[
            pltpu.VMEM((padded, rows, shape[2]), prob.dtype),
            pltpu.SemaphoreType.DMA((2,)),
        ],
        compiler_params=pltpu.CompilerParams(vmem_limit_bytes=VMEM_LIMIT),
        cost_estimate=pl.CostEstimate(
            flops=prob.size * 4, bytes_accessed=prob.size * 4, transcendentals=0
        ),
        name="emit",
    )(prob, *before)


def shifted(block, axis, by):
    devices = lax.axis_size(axis)
    pairs = [(i, i + by) for i in range(devices) if 0 <= i + by < devices]
    return lax.ppermute(block, axis, pairs)


def padded_2(block, sides, width):
    for axis, dim in sides:
        low = shifted(lax.slice_in_dim(block, block.shape[dim] - width, None, axis=dim), axis, 1)
        high = shifted(lax.slice_in_dim(block, 0, width, axis=dim), axis, -1)
        block = jnp.concatenate([low, block, high], axis=dim)
    return block


def gauss_line():
    position = jnp.arange(PATCH, dtype=jnp.float32) - (PATCH - 1) / 2.0
    sigma = 0.125 * PATCH
    return position * position / (2.0 * sigma * sigma)


def gauss_table():
    line = gauss_line()
    table = jnp.exp(-(line[:, None] + line[None, :]))
    return jnp.pad(table, ((0, 0), (0, TILE - PATCH)))


def three_parts(values):
    high = values.astype(jnp.bfloat16)
    rest = values - high.astype(jnp.float32)
    middle = rest.astype(jnp.bfloat16)
    low = (rest - middle.astype(jnp.float32)).astype(jnp.bfloat16)
    return jnp.stack([high, middle, low], axis=1)


def head_matrix(out_weight, out_bias):
    classes, feat = out_weight.shape
    matrix = jnp.concatenate(
        [out_weight, three_parts(out_bias), jnp.zeros((classes, 13), jnp.bfloat16)], axis=1
    )
    return jnp.concatenate([matrix, matrix[-2:]], axis=0)


def ring_of(plane):
    gap = jnp.zeros((plane.shape[0], RING - plane.shape[1]), plane.dtype)
    return jnp.concatenate([plane[:, 2:], gap, plane[:, :2]], axis=1)


def rows_of(plane, first, rows):
    span = plane.shape[0]
    return jnp.concatenate(
        [plane[first : first + rows], plane[span - first - rows : span - first]], axis=0
    )


def on_device(features, patch_ids, patch_count, labels, mlp_weight, mlp_bias, out_weight, out_bias):
    wide, narrow = lax.axis_size("wide"), lax.axis_size("narrow")
    here_wide, here_narrow = lax.axis_index("wide"), lax.axis_index("narrow")
    feat = features.shape[3]
    slots = features.shape[2]
    classes = out_weight.shape[0]
    span_x, span_y = labels.shape
    rows_q = ROWS * narrow
    feats = features[0, 0]

    slot_ids = jnp.arange(slots, dtype=jnp.int32)
    halves = jnp.arange(2, dtype=jnp.int32)
    columns = jnp.arange(2 * wide, dtype=jnp.int32)
    listed = slot_ids < patch_count[0, 0]
    column_of = patch_ids[0, 0][:, None] // rows_q + halves[None, :]
    hit = listed[:, None, None] & (column_of[:, :, None] == columns[None, None, :])
    pick = jnp.max(
        jnp.where(hit, (2 * slot_ids[:, None] + halves[None, :])[:, :, None], -1), axis=(0, 1)
    )

    payloads = [pack(feats, pick, first, rows) for first, rows in CHUNKS]
    received = [
        lax.all_to_all(
            payload.reshape(wide, 2, feat, payload.shape[2]), "wide", 0, 0, tiled=True
        ).reshape(2 * wide, feat, payload.shape[2])
        for payload in payloads
    ]

    kind = (patch_ids[0, 0] % rows_q - ROWS * here_narrow)[:, None] * 2 + halves[None, :]
    tag = jnp.max(jnp.where(hit, kind[:, :, None], -1), axis=(0, 1)).reshape(wide, 2)
    tag = lax.all_to_all(tag, "wide", 0, 0, tiled=True).reshape(-1)
    valid = tag >= 0
    order = jnp.cumsum(valid.astype(jnp.int32)) - 1
    code = jnp.where(valid, columns * 8 + tag, 0)
    place = valid[:, None] & (order[:, None] == columns[None, :])
    codes = jnp.concatenate(
        [
            jnp.sum(jnp.where(place, code[:, None], 0), axis=0),
            jnp.sum(valid.astype(jnp.int32))[None],
        ]
    )

    table = gauss_table()
    line = table[:, :PATCH]
    kinds = jnp.arange(2 * ROWS, dtype=jnp.int32)
    counts = jnp.sum(
        (tag.reshape(wide, 2, 1) == kinds).astype(jnp.float32), axis=0
    ).reshape(2, ROWS, 2)
    square = line.reshape(2, QUAD, PATCH)
    by_row = jnp.sum(
        counts[:, :, :, None, None] * square[None, None], axis=2
    )
    by_row = by_row.transpose(1, 0, 2, 3).reshape(ROWS, span_x, PATCH)
    norm = sum(
        jnp.pad(by_row[i], ((0, 0), (QUAD * i, QUAD * (ROWS - 1 - i)))) for i in range(ROWS)
    )
    came_low = shifted(norm[:, span_y - 2 :], "narrow", 1)
    came_high = shifted(norm[:, :2], "narrow", -1)
    norm = jnp.concatenate(
        [
            came_low[:, :2],
            norm[:, :QUAD] + came_low[:, 2:],
            norm[:, QUAD:span_y],
            norm[:, span_y : span_y + 2] + came_high,
        ],
        axis=1,
    )
    across = ROWS * QUAD * here_narrow - 2 + jnp.arange(span_y + 4, dtype=jnp.int32)
    inside = (across >= 0) & (across < narrow * span_y)
    inverse = ring_of(jnp.where(inside[None, :], 1.0 / (norm + 0.001), 0.0))

    label_wide = padded_2(labels + 1, (("wide", 0), ("narrow", 1)), 2)
    centre = label_wide[1:-1, 1:-1]
    same = (
        (label_wide[:-2, 1:-1] == centre)
        & (label_wide[2:, 1:-1] == centre)
        & (label_wide[1:-1, :-2] == centre)
        & (label_wide[1:-1, 2:] == centre)
    )
    boundary = jnp.where(same, 0, centre)
    boundary = ring_of(jnp.pad(boundary, ((0, 0), (1, 1))))

    head_weight = head_matrix(out_weight, out_bias)
    bias_tile = jnp.broadcast_to(mlp_bias[:, None], (feat, TILE))
    probs = []
    blended = None
    for (first, rows), recv in zip(CHUNKS, received):
        own, up, down = head_of(
            recv, codes, mlp_weight, bias_tile, head_weight, table, first, rows, classes
        )
        up = shifted(up, "narrow", 1)
        down = shifted(down, "narrow", -1)
        prob = blend_of(own, up, down, rows_of(inverse, first, rows))
        probs.append(prob)
        blended = emit(
            prob, first, span_x - first - rows, (classes, span_x, span_y), blended
        )
    edge_rows = CHUNKS[0][1]
    before = shifted(probs[0][2 * edge_rows - 2 :], "wide", 1)
    after = shifted(probs[0][:2], "wide", -1)
    last, last_rows = CHUNKS[-1]
    lows = [prob[:rows] for prob, (_, rows) in zip(probs, CHUNKS)]
    highs = [prob[rows:] for prob, (_, rows) in zip(probs, CHUNKS)]
    low = jnp.concatenate([before] + lows[:-1], axis=0)
    high = jnp.concatenate(highs[:-1][::-1] + [after], axis=0)
    middle = jnp.concatenate([lows[-2][-4:], probs[-1], highs[-2][:4]], axis=0)
    sums = (
        dice_of(low, boundary[:last])
        + dice_of(high, boundary[span_x - last + 2 :])
        + dice_of(middle, boundary[last - 2 : span_x - last + 4])
    )[:, :, 0]
    whole = jnp.broadcast_to(sums[None], (wide * narrow,) + sums.shape)
    whole = jnp.sum(lax.all_to_all(whole, ("wide", "narrow"), 0, 0, tiled=True), axis=0)
    dice = ((whole[0] + 1.0) / (whole[1] + 1.0))[:classes]
    slab_sums = (sums[:, :classes] / jnp.float32(span_x)).reshape(1, 1, 2, classes)
    return (blended, dice, slab_sums)


def solution(mesh):
    return jax.shard_map(
        on_device,
        mesh=mesh,
        in_specs=(
            P("wide", "narrow", None, None, None),
            P("wide", "narrow", None),
            P("wide", "narrow"),
            P("wide", "narrow"),
            P(),
            P(),
            P(),
            P(),
        ),
        out_specs=(P(None, "wide", "narrow"), P(), P("wide", "narrow", None, None)),
        check_vma=False,
    )
```

```python
import functools

import jax
import jax.numpy as jnp
from jax import lax
from jax.experimental import pallas as pl
from jax.experimental.pallas import tpu as pltpu
from jax.sharding import PartitionSpec as P

PATCH = 96
QUAD = 48
TILE = 128
RING = 256
ROWS = 4
CHUNKS = ((0, 16), (16, 16), (32, 16))
VMEM_LIMIT = 50 * 1024 * 1024


def pack_kernel(first, rows, pick_ref, feats_ref, *refs):
    out_ref, sems = refs[-2:]
    width = rows * PATCH

    def copy_of(column):
        source = pick_ref[column]
        start = first if column % 2 == 0 else QUAD - first - rows
        lane = pl.multiple_of((source % 2) * (QUAD * PATCH) + start * PATCH, TILE)
        return pltpu.make_async_copy(
            feats_ref.at[source // 2, :, pl.ds(lane, width)], out_ref.at[column], sems.at[column]
        )

    columns = out_ref.shape[0]
    for column in range(columns):

        @pl.when(pick_ref[column] >= 0)
        def _():
            copy_of(column).start()

    for column in range(columns):

        @pl.when(pick_ref[column] >= 0)
        def _():
            copy_of(column).wait()


def pack(feats, pick, first, rows, *after):
    columns = pick.shape[0]
    width = rows * PATCH
    return pl.pallas_call(
        functools.partial(pack_kernel, first, rows),
        out_shape=jax.ShapeDtypeStruct((columns, feats.shape[1], width), feats.dtype),
        in_specs=[pl.BlockSpec(memory_space=pltpu.SMEM)]
        + [pl.BlockSpec(memory_space=pl.ANY)] * (1 + len(after)),
        out_specs=pl.BlockSpec(memory_space=pltpu.VMEM),
        scratch_shapes=[pltpu.SemaphoreType.DMA((columns,))],
        compiler_params=pltpu.CompilerParams(vmem_limit_bytes=VMEM_LIMIT),
        cost_estimate=pl.CostEstimate(
            flops=0, bytes_accessed=columns * width * feats.shape[1] * 4, transcendentals=0
        ),
        name="pack",
    )(pick, feats, *after)


def spread_rows(tiles, lane):
    one, two, three = tiles
    return (
        one,
        jnp.where(lane < 32, pltpu.roll(one, 32, 1), pltpu.roll(two, 32, 1)),
        jnp.where(lane < 64, pltpu.roll(two, 64, 1), pltpu.roll(three, 64, 1)),
        pltpu.roll(three, 96, 1),
    )


def head_kernel(
    first, rows, classes, code_ref, recv_ref, mlp_ref, bias_ref, head_ref, gauss_ref,
    own_ref, up_ref, down_ref, acc_ref, edge_ref, act_ref,
):
    feat = recv_ref.shape[1]
    padded = head_ref.shape[0]
    lane_feat = lax.broadcasted_iota(jnp.int32, (feat, TILE), 1)
    lane = lax.broadcasted_iota(jnp.int32, (padded, TILE), 1)
    real = lax.broadcasted_iota(jnp.int32, (padded, TILE), 0) < classes
    mlp = mlp_ref[...]
    head = head_ref[...]
    act_ref[feat:, :] = jnp.ones((act_ref.shape[0] - feat, act_ref.shape[1]), jnp.bfloat16)

    @pl.loop(0, ROWS)
    def _(which):
        @pl.loop(0, 2 * rows)
        def _(row):
            acc_ref[which, row] = jnp.zeros((padded, TILE), jnp.float32)

    edge_ref[...] = jnp.zeros_like(edge_ref)

    @pl.loop(0, code_ref[2 * 16])
    def _(item):
        code = code_ref[item]
        slot = code // 8
        which = (code // 2) % 4
        side = slot % 2
        start = (code % 2) * QUAD + jnp.where(side == 0, first, QUAD - first - rows)
        flat = recv_ref[slot]
        hidden = jnp.dot(mlp, flat, preferred_element_type=jnp.float32)
        for group in range(rows // 4):
            tiles = []
            for i in range(3):
                part = slice((group * 3 + i) * TILE, (group * 3 + i + 1) * TILE)
                tiles.append(
                    flat[:, part].astype(jnp.float32)
                    + jnp.maximum(hidden[:, part] + bias_ref[...], 0.0)
                )
            for i, tile in enumerate(spread_rows(tiles, lane_feat)):
                at = (group * 4 + i) * TILE
                act_ref[0:feat, at : at + TILE] = tile.astype(jnp.bfloat16)
        logits = jnp.dot(head, act_ref[...], preferred_element_type=jnp.float32)
        for i in range(rows):
            part = logits[:, i * TILE : (i + 1) * TILE]
            top = jnp.max(part, axis=0, keepdims=True)
            raised = jnp.where(real, jnp.exp(part - top), 0.0)
            scale = gauss_ref[pl.ds(start + i, 1), :] / jnp.sum(raised, axis=0, keepdims=True)
            acc_ref[which, side * rows + i] += (
                (raised * scale).astype(jnp.bfloat16).astype(jnp.float32)
            )

    def merged(row):
        a0, a1, a2, a3 = [acc_ref[which, row] for which in range(ROWS)]
        a1 = pltpu.roll(a1, 48, 1)
        a2 = pltpu.roll(a2, 96, 1)
        low = a0 + jnp.where(lane >= 48, a1, 0.0) + jnp.where(lane >= 96, a2, 0.0)
        high = (
            jnp.where(lane < 48, a1, 0.0)
            + jnp.where(lane < 96, a2, 0.0)
            + pltpu.roll(a3, 16, 1)
        )
        own_ref[row, :, 0:TILE] = low
        own_ref[row, :, TILE:RING] = high
        edge_ref[...] = jnp.where(
            (lane == 2 * row) | (lane == 2 * row + 1), pltpu.roll(low, 2 * row, 1), edge_ref[...]
        )
        return high

    @pl.loop(0, rows)
    def _(pair):
        even = merged(2 * pair)
        odd = merged(2 * pair + 1)
        up_ref[pair] = jnp.where(lane < 64, pltpu.roll(even, 66, 1), pltpu.roll(odd, 2, 1)).astype(
            jnp.bfloat16
        )

    down_ref[...] = edge_ref[...].astype(jnp.bfloat16)


def head_of(recv, codes, mlp_weight, bias_tile, head_weight, gauss, first, rows, classes):
    padded = head_weight.shape[0]
    whole = pl.BlockSpec(memory_space=pltpu.VMEM)
    return pl.pallas_call(
        functools.partial(head_kernel, first, rows, classes),
        out_shape=(
            jax.ShapeDtypeStruct((2 * rows, padded, RING), jnp.float32),
            jax.ShapeDtypeStruct((rows, padded, TILE), jnp.bfloat16),
            jax.ShapeDtypeStruct((padded, TILE), jnp.bfloat16),
        ),
        in_specs=[pl.BlockSpec(memory_space=pltpu.SMEM)] + [whole] * 5,
        out_specs=(whole, whole, whole),
        scratch_shapes=[
            pltpu.VMEM((ROWS, 2 * rows, padded, TILE), jnp.float32),
            pltpu.VMEM((padded, TILE), jnp.float32),
            pltpu.VMEM((head_weight.shape[1], rows * TILE), jnp.bfloat16),
        ],
        compiler_params=pltpu.CompilerParams(vmem_limit_bytes=VMEM_LIMIT),
        cost_estimate=pl.CostEstimate(
            flops=rows * 900_000_000 // 48, bytes_accessed=rows * 25_000_000 // 48,
            transcendentals=rows * 12_000_000 // 48,
        ),
        name="head",
    )(codes, recv, mlp_weight, bias_tile, head_weight, gauss)


def blend_kernel(own_ref, up_ref, down_ref, inv_ref, prob_ref):
    rows, padded, _ = own_ref.shape
    lane = lax.broadcasted_iota(jnp.int32, (padded, TILE), 1)
    first = lax.broadcasted_iota(jnp.int32, (padded, TILE), 0) == 0
    extra = jnp.where(first, 0.001, 0.0)
    down = down_ref[...].astype(jnp.float32)

    def one(row, came, shift):
        came = pltpu.roll(came, shift, 1)
        low = own_ref[row, :, 0:TILE] + jnp.where(lane < 48, came, 0.0)
        high = own_ref[row, :, TILE:RING] + jnp.where(lane >= 126, came, 0.0)
        after = pltpu.roll(down, lax.rem(192 - 2 * row, TILE), 1)
        high = high + jnp.where((lane == 64) | (lane == 65), after, 0.0)
        scale = inv_ref[pl.ds(row, 1), :]
        prob_ref[row, :, 0:TILE] = ((low + extra) * scale[:, 0:TILE]).astype(jnp.bfloat16)
        prob_ref[row, :, TILE:RING] = ((high + extra) * scale[:, TILE:RING]).astype(jnp.bfloat16)

    @pl.loop(0, rows // 2)
    def _(pair):
        came = up_ref[pair].astype(jnp.float32)
        one(2 * pair, came, 126)
        one(2 * pair + 1, came, 62)


def blend_of(own, up, down, inv):
    whole = pl.BlockSpec(memory_space=pltpu.VMEM)
    return pl.pallas_call(
        blend_kernel,
        out_shape=jax.ShapeDtypeStruct(own.shape, jnp.bfloat16),
        in_specs=[whole] * 4,
        out_specs=whole,
        compiler_params=pltpu.CompilerParams(vmem_limit_bytes=VMEM_LIMIT),
        cost_estimate=pl.CostEstimate(
            flops=own.size * 4, bytes_accessed=own.size * 7, transcendentals=0
        ),
        name="blend",
    )(own, up, down, inv)


def turn(tiles, forward, lane):
    low, high = tiles
    shift, at = (1, 0) if forward else (TILE - 1, TILE - 1)
    low, high = pltpu.roll(low, shift, 1), pltpu.roll(high, shift, 1)
    return jnp.where(lane == at, high, low), jnp.where(lane == at, low, high)


def dice_kernel(prob_ref, label_ref, sums_ref, edge_ref, numer_ref, denom_ref):
    padded = prob_ref.shape[1]
    rows = prob_ref.shape[0] - 4
    lane = lax.broadcasted_iota(jnp.int32, (8, TILE), 1)
    klass = lax.broadcasted_iota(jnp.int32, (8, TILE), 0) + 1
    owned = (lane < TILE, lane < 64)

    def tiles_of(ref, row, group):
        return [
            ref[row, group : group + 8, i * TILE : (i + 1) * TILE].astype(jnp.float32)
            for i in range(2)
        ]

    @pl.loop(0, rows + 2)
    def _(row):
        for group in range(0, padded, 8):
            centre = tiles_of(prob_ref, row + 1, group)
            before, after = tiles_of(prob_ref, row, group), tiles_of(prob_ref, row + 2, group)
            left, right = turn(centre, True, lane), turn(centre, False, lane)
            for i in range(2):
                low = jnp.minimum(
                    jnp.minimum(before[i], after[i]), jnp.minimum(left[i], right[i])
                )
                edge_ref[row, group : group + 8, i * TILE : (i + 1) * TILE] = centre[
                    i
                ] - jnp.minimum(centre[i], low)

    numer_ref[...] = jnp.zeros_like(numer_ref)
    denom_ref[...] = jnp.zeros_like(denom_ref)

    @pl.loop(0, rows)
    def _(row):
        def labels_of(at):
            line = label_ref[pl.ds(at, 1), :]
            return [
                jnp.broadcast_to(line[:, i * TILE : (i + 1) * TILE], (8, TILE)) for i in range(2)
            ]

        middle = labels_of(row + 1)
        near = (labels_of(row), labels_of(row + 2), turn(middle, True, lane), turn(middle, False, lane))
        for group in range(0, padded, 8):
            centre = tiles_of(edge_ref, row + 1, group)
            before, after = tiles_of(edge_ref, row, group), tiles_of(edge_ref, row + 2, group)
            left, right = turn(centre, True, lane), turn(centre, False, lane)
            numer = numer_ref[group : group + 8, :]
            denom = denom_ref[group : group + 8, :]
            for i in range(2):
                wide = jnp.maximum(
                    jnp.maximum(centre[i], jnp.maximum(before[i], after[i])),
                    jnp.maximum(left[i], right[i]),
                )
                here = middle[i] == klass + group
                about = here
                for other in near:
                    about = about | (other[i] == klass + group)
                value = jnp.where(about, centre[i], 0.0) + jnp.where(here, wide, 0.0)
                total = centre[i] + jnp.where(here, 1.0, 0.0)
                if i == 1:
                    value = jnp.where(owned[i], value, 0.0)
                    total = jnp.where(owned[i], total, 0.0)
                numer = numer + value
                denom = denom + total
            numer_ref[group : group + 8, :] = numer
            denom_ref[group : group + 8, :] = denom

    sums_ref[0] = jnp.broadcast_to(
        jnp.sum(numer_ref[...], axis=1, keepdims=True), (padded, TILE)
    )
    sums_ref[1] = jnp.broadcast_to(
        jnp.sum(denom_ref[...], axis=1, keepdims=True), (padded, TILE)
    )


def dice_of(prob, label):
    rows, padded, _ = prob.shape
    whole = pl.BlockSpec(memory_space=pltpu.VMEM)
    return pl.pallas_call(
        dice_kernel,
        out_shape=jax.ShapeDtypeStruct((2, padded, TILE), jnp.float32),
        in_specs=[whole] * 2,
        out_specs=whole,
        scratch_shapes=[
            pltpu.VMEM((rows - 2, padded, RING), jnp.float32),
            pltpu.VMEM((padded, TILE), jnp.float32),
            pltpu.VMEM((padded, TILE), jnp.float32),
        ],
        compiler_params=pltpu.CompilerParams(vmem_limit_bytes=VMEM_LIMIT),
        cost_estimate=pl.CostEstimate(
            flops=prob.size * 30, bytes_accessed=prob.size * 2, transcendentals=0
        ),
        name="dice",
    )(prob, label)


def emit_kernel(low, high, prob_ref, *refs):
    out_ref, turned_ref, sems = refs[-3:]
    rows = prob_ref.shape[0]
    _, span_y, classes = out_ref.shape
    half = rows // 2

    def copy_of(i, at):
        return pltpu.make_async_copy(
            turned_ref.at[pl.ds(i * half, half)], out_ref.at[pl.ds(at, half)], sems.at[i]
        )

    for i, at in enumerate((low, high)):

        @pl.loop(0, half)
        def _(index):
            row = i * half + index
            for j in range(2):
                block = prob_ref[row, :, j * TILE : (j + 1) * TILE].astype(jnp.float32)
                block = jnp.transpose(block, (1, 0))
                stop = min((j + 1) * TILE, span_y)
                turned_ref[row, j * TILE : stop, :] = block[
                    : stop - j * TILE, :classes
                ].astype(jnp.bfloat16)

        copy_of(i, at).start()
    for i, at in enumerate((low, high)):
        copy_of(i, at).wait()


def emit(prob, low, high, shape, out=None):
    rows = prob.shape[0]
    anywhere = pl.BlockSpec(memory_space=pl.ANY)
    before = () if out is None else (out,)
    return pl.pallas_call(
        functools.partial(emit_kernel, low, high),
        out_shape=jax.ShapeDtypeStruct(shape, prob.dtype),
        in_specs=[pl.BlockSpec(memory_space=pltpu.VMEM)] + [anywhere] * len(before),
        out_specs=anywhere,
        input_output_aliases={1: 0} if before else {},
        scratch_shapes=[
            pltpu.VMEM((rows,) + shape[1:], prob.dtype),
            pltpu.SemaphoreType.DMA((2,)),
        ],
        compiler_params=pltpu.CompilerParams(vmem_limit_bytes=VMEM_LIMIT),
        cost_estimate=pl.CostEstimate(
            flops=prob.size * 4, bytes_accessed=prob.size * 4, transcendentals=0
        ),
        name="emit",
    )(prob, *before)


def shifted(block, axis, by):
    devices = lax.axis_size(axis)
    pairs = [(i, i + by) for i in range(devices) if 0 <= i + by < devices]
    return lax.ppermute(block, axis, pairs)


def padded_2(block, sides, width):
    for axis, dim in sides:
        low = shifted(lax.slice_in_dim(block, block.shape[dim] - width, None, axis=dim), axis, 1)
        high = shifted(lax.slice_in_dim(block, 0, width, axis=dim), axis, -1)
        block = jnp.concatenate([low, block, high], axis=dim)
    return block


def gauss_line():
    position = jnp.arange(PATCH, dtype=jnp.float32) - (PATCH - 1) / 2.0
    sigma = 0.125 * PATCH
    return position * position / (2.0 * sigma * sigma)


def gauss_table():
    line = gauss_line()
    table = jnp.exp(-(line[:, None] + line[None, :]))
    return jnp.pad(table, ((0, 0), (0, TILE - PATCH)))


def three_parts(values):
    high = values.astype(jnp.bfloat16)
    rest = values - high.astype(jnp.float32)
    middle = rest.astype(jnp.bfloat16)
    low = (rest - middle.astype(jnp.float32)).astype(jnp.bfloat16)
    return jnp.stack([high, middle, low], axis=1)


def head_matrix(out_weight, out_bias):
    classes, feat = out_weight.shape
    matrix = jnp.concatenate(
        [out_weight, three_parts(out_bias), jnp.zeros((classes, 13), jnp.bfloat16)], axis=1
    )
    return jnp.concatenate([matrix, matrix[-2:]], axis=0)


def ring_of(plane):
    gap = jnp.zeros((plane.shape[0], RING - plane.shape[1]), plane.dtype)
    return jnp.concatenate([plane[:, 2:], gap, plane[:, :2]], axis=1)


def rows_of(plane, first, rows):
    span = plane.shape[0]
    return jnp.concatenate(
        [plane[first : first + rows], plane[span - first - rows : span - first]], axis=0
    )


def on_device(features, patch_ids, patch_count, labels, mlp_weight, mlp_bias, out_weight, out_bias):
    wide, narrow = lax.axis_size("wide"), lax.axis_size("narrow")
    here_wide, here_narrow = lax.axis_index("wide"), lax.axis_index("narrow")
    feat = features.shape[3]
    slots = features.shape[2]
    classes = out_weight.shape[0]
    span_x, span_y = labels.shape
    rows_q = ROWS * narrow
    feats = features[0, 0]

    slot_ids = jnp.arange(slots, dtype=jnp.int32)
    halves = jnp.arange(2, dtype=jnp.int32)
    columns = jnp.arange(2 * wide, dtype=jnp.int32)
    listed = slot_ids < patch_count[0, 0]
    column_of = patch_ids[0, 0][:, None] // rows_q + halves[None, :]
    hit = listed[:, None, None] & (column_of[:, :, None] == columns[None, None, :])
    pick = jnp.max(
        jnp.where(hit, (2 * slot_ids[:, None] + halves[None, :])[:, :, None], -1), axis=(0, 1)
    )

    def exchange(chunk, *after):
        payload = pack(feats, pick, *CHUNKS[chunk], *after)
        shape = payload.shape
        payload = payload.reshape((wide, 2) + shape[1:])
        return lax.all_to_all(payload, "wide", 0, 0, tiled=True).reshape(shape)

    received = [exchange(0), exchange(1)]

    kind = (patch_ids[0, 0] % rows_q - ROWS * here_narrow)[:, None] * 2 + halves[None, :]
    tag = jnp.max(jnp.where(hit, kind[:, :, None], -1), axis=(0, 1)).reshape(wide, 2)
    tag = lax.all_to_all(tag, "wide", 0, 0, tiled=True).reshape(-1)
    valid = tag >= 0
    order = jnp.cumsum(valid.astype(jnp.int32)) - 1
    code = jnp.where(valid, columns * 8 + tag, 0)
    place = valid[:, None] & (order[:, None] == columns[None, :])
    codes = jnp.concatenate(
        [
            jnp.sum(jnp.where(place, code[:, None], 0), axis=0),
            jnp.sum(valid.astype(jnp.int32))[None],
        ]
    )

    table = gauss_table()
    line = table[:, :PATCH]
    kinds = jnp.arange(2 * ROWS, dtype=jnp.int32)
    counts = jnp.sum(
        (tag.reshape(wide, 2, 1) == kinds).astype(jnp.float32), axis=0
    ).reshape(2, ROWS, 2)
    square = line.reshape(2, QUAD, PATCH)
    by_row = jnp.sum(
        counts[:, :, :, None, None] * square[None, None], axis=2
    )
    by_row = by_row.transpose(1, 0, 2, 3).reshape(ROWS, span_x, PATCH)
    norm = sum(
        jnp.pad(by_row[i], ((0, 0), (QUAD * i, QUAD * (ROWS - 1 - i)))) for i in range(ROWS)
    )
    came_low = shifted(norm[:, span_y - 2 :], "narrow", 1)
    came_high = shifted(norm[:, :2], "narrow", -1)
    norm = jnp.concatenate(
        [
            came_low[:, :2],
            norm[:, :QUAD] + came_low[:, 2:],
            norm[:, QUAD:span_y],
            norm[:, span_y : span_y + 2] + came_high,
        ],
        axis=1,
    )
    across = ROWS * QUAD * here_narrow - 2 + jnp.arange(span_y + 4, dtype=jnp.int32)
    inside = (across >= 0) & (across < narrow * span_y)
    inverse = ring_of(jnp.where(inside[None, :], 1.0 / (norm + 0.001), 0.0))

    label_wide = padded_2(labels + 1, (("wide", 0), ("narrow", 1)), 2)
    centre = label_wide[1:-1, 1:-1]
    same = (
        (label_wide[:-2, 1:-1] == centre)
        & (label_wide[2:, 1:-1] == centre)
        & (label_wide[1:-1, :-2] == centre)
        & (label_wide[1:-1, 2:] == centre)
    )
    boundary = jnp.where(same, 0, centre)
    boundary = ring_of(jnp.pad(boundary, ((0, 0), (1, 1))))

    head_weight = head_matrix(out_weight, out_bias)
    bias_tile = jnp.broadcast_to(mlp_bias[:, None], (feat, TILE))
    probs = []
    blended = None
    for chunk, (first, rows) in enumerate(CHUNKS):
        own, up, down = head_of(
            received[chunk], codes, mlp_weight, bias_tile, head_weight, table, first, rows, classes
        )
        if chunk + 2 < len(CHUNKS):
            received.append(exchange(chunk + 2, down))
        up = shifted(up, "narrow", 1)
        down = shifted(down, "narrow", -1)
        prob = blend_of(own, up, down, rows_of(inverse, first, rows))
        probs.append(prob)
        blended = emit(
            prob, first, span_x - first - rows, (span_x, span_y, classes), blended
        )
    edge_rows = CHUNKS[0][1]
    before = shifted(probs[0][2 * edge_rows - 2 :], "wide", 1)
    after = shifted(probs[0][:2], "wide", -1)
    last, last_rows = CHUNKS[-1]
    lows = [prob[:rows] for prob, (_, rows) in zip(probs, CHUNKS)]
    highs = [prob[rows:] for prob, (_, rows) in zip(probs, CHUNKS)]
    low = jnp.concatenate([before] + lows[:-1], axis=0)
    high = jnp.concatenate(highs[:-1][::-1] + [after], axis=0)
    middle = jnp.concatenate([lows[-2][-4:], probs[-1], highs[-2][:4]], axis=0)
    sums = (
        dice_of(low, boundary[:last])
        + dice_of(high, boundary[span_x - last + 2 :])
        + dice_of(middle, boundary[last - 2 : span_x - last + 4])
    )[:, :, 0]
    whole = jnp.broadcast_to(sums[None], (wide * narrow,) + sums.shape)
    whole = jnp.sum(lax.all_to_all(whole, ("wide", "narrow"), 0, 0, tiled=True), axis=0)
    dice = ((whole[0] + 1.0) / (whole[1] + 1.0))[:classes]
    slab_sums = (sums[:, :classes] / jnp.float32(span_x)).reshape(1, 1, 2, classes)
    return (blended.transpose(2, 0, 1), dice, slab_sums)


def solution(mesh):
    return jax.shard_map(
        on_device,
        mesh=mesh,
        in_specs=(
            P("wide", "narrow", None, None, None),
            P("wide", "narrow", None),
            P("wide", "narrow"),
            P("wide", "narrow"),
            P(),
            P(),
            P(),
            P(),
        ),
        out_specs=(P(None, "wide", "narrow"), P(), P("wide", "narrow", None, None)),
        check_vma=False,
    )
```

```python
import functools

import jax
import jax.numpy as jnp
from jax import lax
from jax.experimental import pallas as pl
from jax.experimental.pallas import tpu as pltpu
from jax.sharding import PartitionSpec as P

PATCH = 96
QUAD = 48
TILE = 128
RING = 256
ROWS = 4
CHUNKS = ((0, 16), (16, 16), (32, 16))
VMEM_LIMIT = 50 * 1024 * 1024


def pack_kernel(first, rows, pick_ref, feats_ref, *refs):
    out_ref, sems = refs[-2:]
    width = rows * PATCH

    def copy_of(column):
        source = pick_ref[column]
        start = first if column % 2 == 0 else QUAD - first - rows
        lane = pl.multiple_of((source % 2) * (QUAD * PATCH) + start * PATCH, TILE)
        return pltpu.make_async_copy(
            feats_ref.at[source // 2, :, pl.ds(lane, width)], out_ref.at[column], sems.at[column]
        )

    columns = out_ref.shape[0]
    for column in range(columns):

        @pl.when(pick_ref[column] >= 0)
        def _():
            copy_of(column).start()

    for column in range(columns):

        @pl.when(pick_ref[column] >= 0)
        def _():
            copy_of(column).wait()


def pack(feats, pick, first, rows, *after):
    columns = pick.shape[0]
    width = rows * PATCH
    return pl.pallas_call(
        functools.partial(pack_kernel, first, rows),
        out_shape=jax.ShapeDtypeStruct((columns, feats.shape[1], width), feats.dtype),
        in_specs=[pl.BlockSpec(memory_space=pltpu.SMEM)]
        + [pl.BlockSpec(memory_space=pl.ANY)] * (1 + len(after)),
        out_specs=pl.BlockSpec(memory_space=pltpu.VMEM),
        scratch_shapes=[pltpu.SemaphoreType.DMA((columns,))],
        compiler_params=pltpu.CompilerParams(vmem_limit_bytes=VMEM_LIMIT),
        cost_estimate=pl.CostEstimate(
            flops=0, bytes_accessed=columns * width * feats.shape[1] * 4, transcendentals=0
        ),
        name="pack",
    )(pick, feats, *after)


def spread_rows(tiles, lane):
    one, two, three = tiles
    return (
        one,
        jnp.where(lane < 32, pltpu.roll(one, 32, 1), pltpu.roll(two, 32, 1)),
        jnp.where(lane < 64, pltpu.roll(two, 64, 1), pltpu.roll(three, 64, 1)),
        pltpu.roll(three, 96, 1),
    )


def head_kernel(
    first, rows, classes, code_ref, recv_ref, mlp_ref, bias_ref, head_ref, gauss_ref,
    own_ref, up_ref, down_ref, acc_ref, edge_ref, act0_ref, act1_ref, logit0_ref, logit1_ref,
):
    feat = recv_ref.shape[1]
    padded = head_ref.shape[0]
    lane_feat = lax.broadcasted_iota(jnp.int32, (feat, TILE), 1)
    lane = lax.broadcasted_iota(jnp.int32, (padded, TILE), 1)
    real = lax.broadcasted_iota(jnp.int32, (padded, TILE), 0) < classes
    mlp = mlp_ref[...]
    head = head_ref[...]
    for act_ref in (act0_ref, act1_ref):
        act_ref[feat:, :] = jnp.ones((act_ref.shape[0] - feat, rows * TILE), jnp.bfloat16)

    @pl.loop(0, ROWS)
    def _(which):
        @pl.loop(0, 2 * rows)
        def _(row):
            acc_ref[which, row] = jnp.zeros((padded, TILE), jnp.float32)

    edge_ref[...] = jnp.zeros_like(edge_ref)

    count = code_ref[code_ref.shape[0] - 1]

    def raise_logits(item, act_ref, logit_ref):
        flat = recv_ref[code_ref[jnp.minimum(item, count - 1)] // 8]
        hidden = jnp.dot(mlp, flat, preferred_element_type=jnp.float32)
        for group in range(rows // 4):
            tiles = []
            for i in range(3):
                part = slice((group * 3 + i) * TILE, (group * 3 + i + 1) * TILE)
                tiles.append(
                    flat[:, part].astype(jnp.float32)
                    + jnp.maximum(hidden[:, part] + bias_ref[...], 0.0)
                )
            for i, tile in enumerate(spread_rows(tiles, lane_feat)):
                at = (group * 4 + i) * TILE
                act_ref[0:feat, at : at + TILE] = tile.astype(jnp.bfloat16)
        logit_ref[...] = jnp.dot(head, act_ref[...], preferred_element_type=jnp.float32)

    def add_up(item, logit_ref):
        code = code_ref[jnp.minimum(item, count - 1)]
        which = (code // 2) % 4
        side = (code // 8) % 2
        start = (code % 2) * QUAD + jnp.where(side == 0, first, QUAD - first - rows)
        start = jnp.where(item < count, start, PATCH)
        for i in range(rows):
            part = logit_ref[:, i * TILE : (i + 1) * TILE]
            top = jnp.max(part, axis=0, keepdims=True)
            raised = jnp.where(real, jnp.exp(part - top), 0.0)
            scale = gauss_ref[pl.ds(start + i, 1), :] / jnp.sum(raised, axis=0, keepdims=True)
            acc_ref[which, side * rows + i] += (
                (raised * scale).astype(jnp.bfloat16).astype(jnp.float32)
            )

    @pl.when(count > 0)
    def _():
        raise_logits(0, act0_ref, logit0_ref)

        @pl.loop(0, (count + 1) // 2)
        def _(pair):
            raise_logits(2 * pair + 1, act1_ref, logit1_ref)
            add_up(2 * pair, logit0_ref)
            raise_logits(2 * pair + 2, act0_ref, logit0_ref)
            add_up(2 * pair + 1, logit1_ref)

    def merged(row):
        a0, a1, a2, a3 = [acc_ref[which, row] for which in range(ROWS)]
        a1 = pltpu.roll(a1, 48, 1)
        a2 = pltpu.roll(a2, 96, 1)
        low = a0 + jnp.where(lane >= 48, a1, 0.0) + jnp.where(lane >= 96, a2, 0.0)
        high = (
            jnp.where(lane < 48, a1, 0.0)
            + jnp.where(lane < 96, a2, 0.0)
            + pltpu.roll(a3, 16, 1)
        )
        own_ref[row, :, 0:TILE] = low
        own_ref[row, :, TILE:RING] = high
        edge_ref[...] = jnp.where(
            (lane == 2 * row) | (lane == 2 * row + 1), pltpu.roll(low, 2 * row, 1), edge_ref[...]
        )
        return high

    @pl.loop(0, rows)
    def _(pair):
        even = merged(2 * pair)
        odd = merged(2 * pair + 1)
        up_ref[pair] = jnp.where(lane < 64, pltpu.roll(even, 66, 1), pltpu.roll(odd, 2, 1)).astype(
            jnp.bfloat16
        )

    down_ref[...] = edge_ref[...].astype(jnp.bfloat16)


def head_of(recv, codes, mlp_weight, bias_tile, head_weight, gauss, first, rows, classes):
    padded = head_weight.shape[0]
    whole = pl.BlockSpec(memory_space=pltpu.VMEM)
    return pl.pallas_call(
        functools.partial(head_kernel, first, rows, classes),
        out_shape=(
            jax.ShapeDtypeStruct((2 * rows, padded, RING), jnp.float32),
            jax.ShapeDtypeStruct((rows, padded, TILE), jnp.bfloat16),
            jax.ShapeDtypeStruct((padded, TILE), jnp.bfloat16),
        ),
        in_specs=[pl.BlockSpec(memory_space=pltpu.SMEM)] + [whole] * 5,
        out_specs=(whole, whole, whole),
        scratch_shapes=[
            pltpu.VMEM((ROWS, 2 * rows, padded, TILE), jnp.float32),
            pltpu.VMEM((padded, TILE), jnp.float32),
            pltpu.VMEM((head_weight.shape[1], rows * TILE), jnp.bfloat16),
            pltpu.VMEM((head_weight.shape[1], rows * TILE), jnp.bfloat16),
            pltpu.VMEM((padded, rows * TILE), jnp.float32),
            pltpu.VMEM((padded, rows * TILE), jnp.float32),
        ],
        compiler_params=pltpu.CompilerParams(vmem_limit_bytes=VMEM_LIMIT),
        cost_estimate=pl.CostEstimate(
            flops=rows * 900_000_000 // 48, bytes_accessed=rows * 25_000_000 // 48,
            transcendentals=rows * 12_000_000 // 48,
        ),
        name="head",
    )(codes, recv, mlp_weight, bias_tile, head_weight, gauss)


def blend_kernel(own_ref, up_ref, down_ref, inv_ref, prob_ref):
    rows, padded, _ = own_ref.shape
    lane = lax.broadcasted_iota(jnp.int32, (padded, TILE), 1)
    first = lax.broadcasted_iota(jnp.int32, (padded, TILE), 0) == 0
    extra = jnp.where(first, 0.001, 0.0)
    down = down_ref[...].astype(jnp.float32)

    def one(row, came, shift):
        came = pltpu.roll(came, shift, 1)
        low = own_ref[row, :, 0:TILE] + jnp.where(lane < 48, came, 0.0)
        high = own_ref[row, :, TILE:RING] + jnp.where(lane >= 126, came, 0.0)
        after = pltpu.roll(down, lax.rem(192 - 2 * row, TILE), 1)
        high = high + jnp.where((lane == 64) | (lane == 65), after, 0.0)
        scale = inv_ref[pl.ds(row, 1), :]
        prob_ref[row, :, 0:TILE] = ((low + extra) * scale[:, 0:TILE]).astype(jnp.bfloat16)
        prob_ref[row, :, TILE:RING] = ((high + extra) * scale[:, TILE:RING]).astype(jnp.bfloat16)

    @pl.loop(0, rows // 2)
    def _(pair):
        came = up_ref[pair].astype(jnp.float32)
        one(2 * pair, came, 126)
        one(2 * pair + 1, came, 62)


def blend_of(own, up, down, inv):
    whole = pl.BlockSpec(memory_space=pltpu.VMEM)
    return pl.pallas_call(
        blend_kernel,
        out_shape=jax.ShapeDtypeStruct(own.shape, jnp.bfloat16),
        in_specs=[whole] * 4,
        out_specs=whole,
        compiler_params=pltpu.CompilerParams(vmem_limit_bytes=VMEM_LIMIT),
        cost_estimate=pl.CostEstimate(
            flops=own.size * 4, bytes_accessed=own.size * 7, transcendentals=0
        ),
        name="blend",
    )(own, up, down, inv)


def turn(tiles, forward, lane):
    low, high = tiles
    shift, at = (1, 0) if forward else (TILE - 1, TILE - 1)
    low, high = pltpu.roll(low, shift, 1), pltpu.roll(high, shift, 1)
    return jnp.where(lane == at, high, low), jnp.where(lane == at, low, high)


def dice_kernel(prob_ref, label_ref, sums_ref, edge_ref, numer_ref, denom_ref):
    padded = prob_ref.shape[1]
    rows = prob_ref.shape[0] - 4
    lane = lax.broadcasted_iota(jnp.int32, (8, TILE), 1)
    klass = lax.broadcasted_iota(jnp.int32, (8, TILE), 0) + 1
    owned = (lane < TILE, lane < 64)

    def tiles_of(ref, row, group):
        return [
            ref[row, group : group + 8, i * TILE : (i + 1) * TILE].astype(jnp.float32)
            for i in range(2)
        ]

    @pl.loop(0, rows + 2)
    def _(row):
        for group in range(0, padded, 8):
            centre = tiles_of(prob_ref, row + 1, group)
            before, after = tiles_of(prob_ref, row, group), tiles_of(prob_ref, row + 2, group)
            left, right = turn(centre, True, lane), turn(centre, False, lane)
            for i in range(2):
                low = jnp.minimum(
                    jnp.minimum(before[i], after[i]), jnp.minimum(left[i], right[i])
                )
                edge_ref[row, group : group + 8, i * TILE : (i + 1) * TILE] = centre[
                    i
                ] - jnp.minimum(centre[i], low)

    numer_ref[...] = jnp.zeros_like(numer_ref)
    denom_ref[...] = jnp.zeros_like(denom_ref)

    @pl.loop(0, rows)
    def _(row):
        def labels_of(at):
            line = label_ref[pl.ds(at, 1), :]
            return [
                jnp.broadcast_to(line[:, i * TILE : (i + 1) * TILE], (8, TILE)) for i in range(2)
            ]

        middle = labels_of(row + 1)
        near = (labels_of(row), labels_of(row + 2), turn(middle, True, lane), turn(middle, False, lane))
        for group in range(0, padded, 8):
            centre = tiles_of(edge_ref, row + 1, group)
            before, after = tiles_of(edge_ref, row, group), tiles_of(edge_ref, row + 2, group)
            left, right = turn(centre, True, lane), turn(centre, False, lane)
            numer = numer_ref[group : group + 8, :]
            denom = denom_ref[group : group + 8, :]
            for i in range(2):
                wide = jnp.maximum(
                    jnp.maximum(centre[i], jnp.maximum(before[i], after[i])),
                    jnp.maximum(left[i], right[i]),
                )
                here = middle[i] == klass + group
                about = here
                for other in near:
                    about = about | (other[i] == klass + group)
                value = jnp.where(about, centre[i], 0.0) + jnp.where(here, wide, 0.0)
                total = centre[i] + jnp.where(here, 1.0, 0.0)
                if i == 1:
                    value = jnp.where(owned[i], value, 0.0)
                    total = jnp.where(owned[i], total, 0.0)
                numer = numer + value
                denom = denom + total
            numer_ref[group : group + 8, :] = numer
            denom_ref[group : group + 8, :] = denom

    sums_ref[0] = jnp.broadcast_to(
        jnp.sum(numer_ref[...], axis=1, keepdims=True), (padded, TILE)
    )
    sums_ref[1] = jnp.broadcast_to(
        jnp.sum(denom_ref[...], axis=1, keepdims=True), (padded, TILE)
    )


def dice_of(prob, label):
    rows, padded, _ = prob.shape
    whole = pl.BlockSpec(memory_space=pltpu.VMEM)
    return pl.pallas_call(
        dice_kernel,
        out_shape=jax.ShapeDtypeStruct((2, padded, TILE), jnp.float32),
        in_specs=[whole] * 2,
        out_specs=whole,
        scratch_shapes=[
            pltpu.VMEM((rows - 2, padded, RING), jnp.float32),
            pltpu.VMEM((padded, TILE), jnp.float32),
            pltpu.VMEM((padded, TILE), jnp.float32),
        ],
        compiler_params=pltpu.CompilerParams(vmem_limit_bytes=VMEM_LIMIT),
        cost_estimate=pl.CostEstimate(
            flops=prob.size * 30, bytes_accessed=prob.size * 2, transcendentals=0
        ),
        name="dice",
    )(prob, label)


def emit_kernel(chunks, *refs):
    prob_refs = refs[: len(chunks)]
    out_ref, turned_ref, sems = refs[-3:]
    _, span_y, classes = out_ref.shape
    span_x = out_ref.shape[0]

    copies = []
    base = 0
    for prob_ref, (first, rows) in zip(prob_refs, chunks):
        for i, at in enumerate((first, span_x - first - rows)):

            @pl.loop(0, rows)
            def _(index):
                for j in range(2):
                    block = prob_ref[i * rows + index, :, j * TILE : (j + 1) * TILE]
                    block = jnp.transpose(block.astype(jnp.float32), (1, 0))
                    stop = min((j + 1) * TILE, span_y)
                    turned_ref[base + index, j * TILE : stop, :] = block[
                        : stop - j * TILE, :classes
                    ].astype(jnp.bfloat16)

            copy = pltpu.make_async_copy(
                turned_ref.at[pl.ds(base, rows)], out_ref.at[pl.ds(at, rows)], sems.at[len(copies)]
            )
            copy.start()
            copies.append(copy)
            base += rows
    for copy in copies:
        copy.wait()


def emit(probs, chunks, shape, *before):
    anywhere = pl.BlockSpec(memory_space=pl.ANY)
    rows = sum(prob.shape[0] for prob in probs)
    size = sum(prob.size for prob in probs)
    return pl.pallas_call(
        functools.partial(emit_kernel, chunks),
        out_shape=jax.ShapeDtypeStruct(shape, probs[0].dtype),
        in_specs=[pl.BlockSpec(memory_space=pltpu.VMEM)] * len(probs) + [anywhere] * len(before),
        out_specs=anywhere,
        input_output_aliases={len(probs): 0} if before else {},
        scratch_shapes=[
            pltpu.VMEM((rows,) + shape[1:], probs[0].dtype),
            pltpu.SemaphoreType.DMA((2 * len(chunks),)),
        ],
        compiler_params=pltpu.CompilerParams(vmem_limit_bytes=VMEM_LIMIT),
        cost_estimate=pl.CostEstimate(
            flops=size * 4, bytes_accessed=size * 4, transcendentals=0
        ),
        name="emit",
    )(*probs, *before)


def shifted(block, axis, by):
    devices = lax.axis_size(axis)
    pairs = [(i, i + by) for i in range(devices) if 0 <= i + by < devices]
    return lax.ppermute(block, axis, pairs)


def gauss_line():
    position = jnp.arange(PATCH, dtype=jnp.float32) - (PATCH - 1) / 2.0
    sigma = 0.125 * PATCH
    return position * position / (2.0 * sigma * sigma)


def gauss_table():
    line = gauss_line()
    table = jnp.exp(-(line[:, None] + line[None, :]))
    return jnp.pad(table, ((0, QUAD), (0, TILE - PATCH)))


def three_parts(values):
    high = values.astype(jnp.bfloat16)
    rest = values - high.astype(jnp.float32)
    middle = rest.astype(jnp.bfloat16)
    low = (rest - middle.astype(jnp.float32)).astype(jnp.bfloat16)
    return jnp.stack([high, middle, low], axis=1)


def head_matrix(out_weight, out_bias):
    classes, feat = out_weight.shape
    matrix = jnp.concatenate(
        [out_weight, three_parts(out_bias), jnp.zeros((classes, 13), jnp.bfloat16)], axis=1
    )
    return jnp.concatenate([matrix, matrix[-2:]], axis=0)


def ring_of(plane):
    gap = jnp.zeros((plane.shape[0], RING - plane.shape[1]), plane.dtype)
    return jnp.concatenate([plane[:, 2:], gap, plane[:, :2]], axis=1)


def rows_of(plane, first, rows):
    span = plane.shape[0]
    return jnp.concatenate(
        [plane[first : first + rows], plane[span - first - rows : span - first]], axis=0
    )


def on_device(features, patch_ids, patch_count, labels, mlp_weight, mlp_bias, out_weight, out_bias):
    wide, narrow = lax.axis_size("wide"), lax.axis_size("narrow")
    here_wide, here_narrow = lax.axis_index("wide"), lax.axis_index("narrow")
    feat = features.shape[3]
    slots = features.shape[2]
    classes = out_weight.shape[0]
    span_x, span_y = labels.shape
    rows_q = ROWS * narrow
    feats = features[0, 0]

    slot_ids = jnp.arange(slots, dtype=jnp.int32)
    halves = jnp.arange(2, dtype=jnp.int32)
    columns = jnp.arange(2 * wide, dtype=jnp.int32)
    listed = slot_ids < patch_count[0, 0]
    column_of = patch_ids[0, 0][:, None] // rows_q + halves[None, :]
    hit = listed[:, None, None] & (column_of[:, :, None] == columns[None, None, :])
    pick = jnp.max(
        jnp.where(hit, (2 * slot_ids[:, None] + halves[None, :])[:, :, None], -1), axis=(0, 1)
    )

    def exchange(chunk, *after):
        payload = pack(feats, pick, *CHUNKS[chunk], *after)
        shape = payload.shape
        payload = payload.reshape((wide, 2) + shape[1:])
        return lax.all_to_all(payload, "wide", 0, 0, tiled=True).reshape(shape)

    received = [exchange(0), exchange(1)]

    kind = (patch_ids[0, 0] % rows_q - ROWS * here_narrow)[:, None] * 2 + halves[None, :]
    tag = jnp.max(jnp.where(hit, kind[:, :, None], -1), axis=(0, 1)).reshape(wide, 2)
    marked = labels + 1
    others = jnp.arange(wide, dtype=jnp.int32)[:, None]
    edges = jnp.where(others == here_wide + 1, marked[span_x - 2 :].reshape(1, -1), 0)
    edges = jnp.where(others == here_wide - 1, marked[:2].reshape(1, -1), edges)
    notes = lax.all_to_all(
        jnp.concatenate([tag, edges], axis=1), "wide", 0, 0, tiled=True
    )
    tag = notes[:, :2].reshape(-1)

    def rows_from(device):
        return jnp.sum(jnp.where(others == device, notes[:, 2:], 0), axis=0).reshape(2, span_y)

    label_wide = jnp.concatenate(
        [rows_from(here_wide - 1), marked, rows_from(here_wide + 1)], axis=0
    )
    valid = tag >= 0
    order = jnp.cumsum(valid.astype(jnp.int32)) - 1
    code = jnp.where(valid, columns * 8 + tag, 0)
    place = valid[:, None] & (order[:, None] == columns[None, :])
    codes = jnp.concatenate(
        [
            jnp.sum(jnp.where(place, code[:, None], 0), axis=0),
            jnp.sum(valid.astype(jnp.int32))[None],
        ]
    )

    table = gauss_table()
    square = table[:PATCH, :PATCH].reshape(2, QUAD, PATCH)
    kinds = jnp.arange(2 * ROWS, dtype=jnp.int32)
    counts = jnp.sum((tag.reshape(wide, 2, 1) == kinds).astype(jnp.float32), axis=0)

    def beside(columns, by):
        block = jnp.concatenate(
            [columns.astype(jnp.float32), counts.reshape(2 * ROWS, 2)], axis=0
        )
        return shifted(block, "narrow", by)

    def parts_of(block):
        return block[:-2 * ROWS].astype(jnp.int32), block[-2 * ROWS :].reshape(2, 2 * ROWS)

    blocks = beside(label_wide[:, span_y - 2 :], 1), beside(label_wide[:, :2], -1)
    head_weight = head_matrix(out_weight, out_bias)
    bias_tile = jnp.broadcast_to(mlp_bias[:, None], (feat, TILE))

    def head_at(chunk):
        return head_of(
            received[chunk], codes, mlp_weight, bias_tile, head_weight, table, *CHUNKS[chunk], classes
        )

    heads = [head_at(0)]
    received.append(exchange(2, heads[0][2]))
    heads.append(head_at(1))
    _, low_block, high_block = lax.optimization_barrier((heads[1][2],) + blocks)
    label_low, counts_low = parts_of(low_block)
    label_high, counts_high = parts_of(high_block)

    def plane_of(counts, row):
        pairs = counts.reshape(2, ROWS, 2)[:, row, :, None, None]
        return jnp.sum(pairs * square[None], axis=1).reshape(span_x, PATCH)

    norm = sum(
        jnp.pad(plane_of(counts, i), ((0, 0), (QUAD * i, QUAD * (ROWS - 1 - i))))
        for i in range(ROWS)
    )
    came = plane_of(counts_low, 3)
    norm = jnp.concatenate(
        [
            came[:, 46:48] + plane_of(counts_low, 2)[:, 94:96],
            norm[:, :QUAD] + came[:, 48:],
            norm[:, QUAD:span_y],
            norm[:, span_y : span_y + 2] + plane_of(counts_high, 0)[:, :2],
        ],
        axis=1,
    )
    across = ROWS * QUAD * here_narrow - 2 + jnp.arange(span_y + 4, dtype=jnp.int32)
    inside = (across >= 0) & (across < narrow * span_y)
    inverse = ring_of(jnp.where(inside[None, :], 1.0 / (norm + 0.001), 0.0))

    label_wide = jnp.concatenate([label_low, label_wide, label_high], axis=1)
    centre = label_wide[1:-1, 1:-1]
    same = (
        (label_wide[:-2, 1:-1] == centre)
        & (label_wide[2:, 1:-1] == centre)
        & (label_wide[1:-1, :-2] == centre)
        & (label_wide[1:-1, 2:] == centre)
    )
    boundary = jnp.where(same, 0, centre)
    boundary = ring_of(jnp.pad(boundary, ((0, 0), (1, 1))))

    probs = []
    for chunk, (first, rows) in enumerate(CHUNKS):
        own, up, down = heads[chunk] if chunk < 2 else head_at(chunk)
        up = shifted(up, "narrow", 1)
        down = shifted(down, "narrow", -1)
        prob = blend_of(own, up, down, rows_of(inverse, first, rows))
        probs.append(prob)
    edge_rows = CHUNKS[0][1]
    before = shifted(probs[0][2 * edge_rows - 2 :], "wide", 1)
    after = shifted(probs[0][:2], "wide", -1)
    last, last_rows = CHUNKS[-1]
    lows = [prob[:rows] for prob, (_, rows) in zip(probs, CHUNKS)]
    highs = [prob[rows:] for prob, (_, rows) in zip(probs, CHUNKS)]
    low = jnp.concatenate([before] + lows[:-1], axis=0)
    high = jnp.concatenate(highs[:-1][::-1] + [after], axis=0)
    middle = jnp.concatenate([lows[-2][-4:], probs[-1], highs[-2][:4]], axis=0)
    sums = (
        dice_of(low, boundary[:last])
        + dice_of(high, boundary[span_x - last + 2 :])
        + dice_of(middle, boundary[last - 2 : span_x - last + 4])
    )[:, :, 0]
    shape = (span_x, span_y, classes)
    blended = emit(probs[:1], CHUNKS[:1], shape)
    blended = emit(probs[1:], CHUNKS[1:], shape, blended)
    whole = jnp.broadcast_to(sums[None], (wide * narrow,) + sums.shape)
    whole = jnp.sum(lax.all_to_all(whole, ("wide", "narrow"), 0, 0, tiled=True), axis=0)
    dice = ((whole[0] + 1.0) / (whole[1] + 1.0))[:classes]
    slab_sums = (sums[:, :classes] / jnp.float32(span_x)).reshape(1, 1, 2, classes)
    return (blended.transpose(2, 0, 1), dice, slab_sums)


def solution(mesh):
    return jax.shard_map(
        on_device,
        mesh=mesh,
        in_specs=(
            P("wide", "narrow", None, None, None),
            P("wide", "narrow", None),
            P("wide", "narrow"),
            P("wide", "narrow"),
            P(),
            P(),
            P(),
            P(),
        ),
        out_specs=(P(None, "wide", "narrow"), P(), P("wide", "narrow", None, None)),
        check_vma=False,
    )
```

```python
import functools

import jax
import jax.numpy as jnp
from jax import lax
from jax.experimental import pallas as pl
from jax.experimental.pallas import tpu as pltpu
from jax.sharding import PartitionSpec as P

PATCH = 96
QUAD = 48
TILE = 128
RING = 256
ROWS = 4
CHUNKS = ((0, 12), (12, 20), (32, 16))
VMEM_LIMIT = 50 * 1024 * 1024


def pack_kernel(first, rows, pick_ref, feats_ref, *refs):
    out_ref, sems = refs[-2:]
    width = rows * PATCH

    def copy_of(column):
        source = pick_ref[column]
        start = first if column % 2 == 0 else QUAD - first - rows
        lane = pl.multiple_of((source % 2) * (QUAD * PATCH) + start * PATCH, TILE)
        return pltpu.make_async_copy(
            feats_ref.at[source // 2, :, pl.ds(lane, width)], out_ref.at[column], sems.at[column]
        )

    columns = out_ref.shape[0]
    for column in range(columns):

        @pl.when(pick_ref[column] >= 0)
        def _():
            copy_of(column).start()

    for column in range(columns):

        @pl.when(pick_ref[column] >= 0)
        def _():
            copy_of(column).wait()


def pack(feats, pick, first, rows, *after):
    columns = pick.shape[0]
    width = rows * PATCH
    return pl.pallas_call(
        functools.partial(pack_kernel, first, rows),
        out_shape=jax.ShapeDtypeStruct((columns, feats.shape[1], width), feats.dtype),
        in_specs=[pl.BlockSpec(memory_space=pltpu.SMEM)]
        + [pl.BlockSpec(memory_space=pl.ANY)] * (1 + len(after)),
        out_specs=pl.BlockSpec(memory_space=pltpu.VMEM),
        scratch_shapes=[pltpu.SemaphoreType.DMA((columns,))],
        compiler_params=pltpu.CompilerParams(vmem_limit_bytes=VMEM_LIMIT),
        cost_estimate=pl.CostEstimate(
            flops=0, bytes_accessed=columns * width * feats.shape[1] * 4, transcendentals=0
        ),
        name="pack",
    )(pick, feats, *after)


def spread_rows(tiles, lane):
    one, two, three = tiles
    return (
        one,
        jnp.where(lane < 32, pltpu.roll(one, 32, 1), pltpu.roll(two, 32, 1)),
        jnp.where(lane < 64, pltpu.roll(two, 64, 1), pltpu.roll(three, 64, 1)),
        pltpu.roll(three, 96, 1),
    )


def head_kernel(
    first, rows, classes, code_ref, recv_ref, mlp_ref, bias_ref, head_ref, gauss_ref,
    own_ref, up_ref, down_ref, acc_ref, edge_ref, act0_ref, act1_ref, logit0_ref, logit1_ref,
    half_ref, half_sems, merged_ref, merged_sems,
):
    feat = recv_ref.shape[1]
    padded = head_ref.shape[0]
    lane_feat = lax.broadcasted_iota(jnp.int32, (feat, TILE), 1)
    lane = lax.broadcasted_iota(jnp.int32, (padded, TILE), 1)
    real = lax.broadcasted_iota(jnp.int32, (padded, TILE), 0) < classes
    mlp = mlp_ref[...]
    head = head_ref[...]
    count = code_ref[code_ref.shape[0] - 1]

    def half_copy(item):
        return pltpu.make_async_copy(
            recv_ref.at[code_ref[item] // 8], half_ref.at[item], half_sems.at[item]
        )

    def arrived(item):
        @pl.when(item < count)
        def _():
            half_copy(item).wait()

    @pl.loop(0, count)
    def _(item):
        half_copy(item).start()

    for act_ref in (act0_ref, act1_ref):
        act_ref[feat:, :] = jnp.ones((act_ref.shape[0] - feat, rows * TILE), jnp.bfloat16)

    @pl.loop(0, ROWS)
    def _(which):
        @pl.loop(0, 2 * rows)
        def _(row):
            acc_ref[which, row] = jnp.zeros((padded, TILE), jnp.float32)

    edge_ref[...] = jnp.zeros_like(edge_ref)

    def raise_logits(item, act_ref, logit_ref):
        flat = half_ref[jnp.minimum(item, count - 1)]
        hidden = jnp.dot(mlp, flat, preferred_element_type=jnp.float32)
        for group in range(rows // 4):
            tiles = []
            for i in range(3):
                part = slice((group * 3 + i) * TILE, (group * 3 + i + 1) * TILE)
                tiles.append(
                    flat[:, part].astype(jnp.float32)
                    + jnp.maximum(hidden[:, part] + bias_ref[...], 0.0)
                )
            for i, tile in enumerate(spread_rows(tiles, lane_feat)):
                at = (group * 4 + i) * TILE
                act_ref[0:feat, at : at + TILE] = tile.astype(jnp.bfloat16)
        logit_ref[...] = jnp.dot(head, act_ref[...], preferred_element_type=jnp.float32)

    def add_up(item, logit_ref):
        code = code_ref[jnp.minimum(item, count - 1)]
        which = (code // 2) % 4
        side = (code // 8) % 2
        start = (code % 2) * QUAD + jnp.where(side == 0, first, QUAD - first - rows)
        start = jnp.where(item < count, start, PATCH)
        for i in range(rows):
            part = logit_ref[:, i * TILE : (i + 1) * TILE]
            top = jnp.max(part, axis=0, keepdims=True)
            raised = jnp.where(real, jnp.exp(part - top), 0.0)
            scale = gauss_ref[pl.ds(start + i, 1), :] / jnp.sum(raised, axis=0, keepdims=True)
            acc_ref[which, side * rows + i] += (
                (raised * scale).astype(jnp.bfloat16).astype(jnp.float32)
            )

    @pl.when(count > 0)
    def _():
        arrived(0)
        raise_logits(0, act0_ref, logit0_ref)

        @pl.loop(0, (count + 1) // 2)
        def _(pair):
            arrived(2 * pair + 1)
            arrived(2 * pair + 2)
            raise_logits(2 * pair + 1, act1_ref, logit1_ref)
            add_up(2 * pair, logit0_ref)
            raise_logits(2 * pair + 2, act0_ref, logit0_ref)
            add_up(2 * pair + 1, logit1_ref)

    def merged(row):
        a0, a1, a2, a3 = [acc_ref[which, row] for which in range(ROWS)]
        a1 = pltpu.roll(a1, 48, 1)
        a2 = pltpu.roll(a2, 96, 1)
        low = a0 + jnp.where(lane >= 48, a1, 0.0) + jnp.where(lane >= 96, a2, 0.0)
        high = (
            jnp.where(lane < 48, a1, 0.0)
            + jnp.where(lane < 96, a2, 0.0)
            + pltpu.roll(a3, 16, 1)
        )
        merged_ref[row, :, 0:TILE] = low
        merged_ref[row, :, TILE:RING] = high
        edge_ref[...] = jnp.where(
            (lane == 2 * row) | (lane == 2 * row + 1), pltpu.roll(low, 2 * row, 1), edge_ref[...]
        )
        return high

    def own_copy(pair):
        place = pl.ds(2 * pair, 2)
        return pltpu.make_async_copy(
            merged_ref.at[place], own_ref.at[place], merged_sems.at[pair]
        )

    @pl.loop(0, rows)
    def _(pair):
        even = merged(2 * pair)
        odd = merged(2 * pair + 1)
        own_copy(pair).start()
        up_ref[pair] = jnp.where(lane < 64, pltpu.roll(even, 66, 1), pltpu.roll(odd, 2, 1)).astype(
            jnp.bfloat16
        )

    @pl.loop(0, rows)
    def _(pair):
        own_copy(pair).wait()

    down_ref[...] = edge_ref[...].astype(jnp.bfloat16)


def head_of(recv, codes, mlp_weight, bias_tile, head_weight, gauss, first, rows, classes):
    padded = head_weight.shape[0]
    whole = pl.BlockSpec(memory_space=pltpu.VMEM)
    return pl.pallas_call(
        functools.partial(head_kernel, first, rows, classes),
        out_shape=(
            jax.ShapeDtypeStruct((2 * rows, padded, RING), jnp.float32),
            jax.ShapeDtypeStruct((rows, padded, TILE), jnp.bfloat16),
            jax.ShapeDtypeStruct((padded, TILE), jnp.bfloat16),
        ),
        in_specs=[
            pl.BlockSpec(memory_space=pltpu.SMEM), pl.BlockSpec(memory_space=pl.ANY)
        ]
        + [whole] * 4,
        out_specs=(pl.BlockSpec(memory_space=pl.ANY), whole, whole),
        scratch_shapes=[
            pltpu.VMEM((ROWS, 2 * rows, padded, TILE), jnp.float32),
            pltpu.VMEM((padded, TILE), jnp.float32),
            pltpu.VMEM((head_weight.shape[1], rows * TILE), jnp.bfloat16),
            pltpu.VMEM((head_weight.shape[1], rows * TILE), jnp.bfloat16),
            pltpu.VMEM((padded, rows * TILE), jnp.float32),
            pltpu.VMEM((padded, rows * TILE), jnp.float32),
            pltpu.VMEM(recv.shape, recv.dtype),
            pltpu.SemaphoreType.DMA(recv.shape[:1]),
            pltpu.VMEM((2 * rows, padded, RING), jnp.float32),
            pltpu.SemaphoreType.DMA((rows,)),
        ],
        compiler_params=pltpu.CompilerParams(vmem_limit_bytes=VMEM_LIMIT),
        cost_estimate=pl.CostEstimate(
            flops=rows * 900_000_000 // 48, bytes_accessed=rows * 25_000_000 // 48,
            transcendentals=rows * 12_000_000 // 48,
        ),
        name="head",
    )(codes, recv, mlp_weight, bias_tile, head_weight, gauss)


def blend_kernel(own_ref, up_ref, down_ref, inv_ref, prob_ref):
    rows, padded, _ = own_ref.shape
    lane = lax.broadcasted_iota(jnp.int32, (padded, TILE), 1)
    first = lax.broadcasted_iota(jnp.int32, (padded, TILE), 0) == 0
    extra = jnp.where(first, 0.001, 0.0)
    down = down_ref[...].astype(jnp.float32)
    base = pl.program_id(0) * rows

    for row in range(rows):
        came = up_ref[row // 2].astype(jnp.float32)
        came = pltpu.roll(came, 126 if row % 2 == 0 else 62, 1)
        low = own_ref[row, :, 0:TILE] + jnp.where(lane < 48, came, 0.0)
        high = own_ref[row, :, TILE:RING] + jnp.where(lane >= 126, came, 0.0)
        after = pltpu.roll(down, lax.rem(192 - 2 * (base + row), TILE), 1)
        high = high + jnp.where((lane == 64) | (lane == 65), after, 0.0)
        scale = inv_ref[pl.ds(base + row, 1), :]
        prob_ref[row, :, 0:TILE] = ((low + extra) * scale[:, 0:TILE]).astype(jnp.bfloat16)
        prob_ref[row, :, TILE:RING] = ((high + extra) * scale[:, TILE:RING]).astype(jnp.bfloat16)


def blend_of(own, up, down, inv):
    rows, padded, _ = own.shape
    whole = pl.BlockSpec(memory_space=pltpu.VMEM)
    step = 8
    return pl.pallas_call(
        blend_kernel,
        grid=(rows // step,),
        out_shape=jax.ShapeDtypeStruct(own.shape, jnp.bfloat16),
        in_specs=[
            pl.BlockSpec((step, padded, RING), lambda i: (i, 0, 0)),
            pl.BlockSpec((step // 2, padded, TILE), lambda i: (i, 0, 0)),
            whole,
            whole,
        ],
        out_specs=pl.BlockSpec((step, padded, RING), lambda i: (i, 0, 0)),
        compiler_params=pltpu.CompilerParams(vmem_limit_bytes=VMEM_LIMIT),
        cost_estimate=pl.CostEstimate(
            flops=own.size * 4, bytes_accessed=own.size * 7, transcendentals=0
        ),
        name="blend",
    )(own, up, down, inv)


def turn(tiles, forward, lane):
    low, high = tiles
    shift, at = (1, 0) if forward else (TILE - 1, TILE - 1)
    low, high = pltpu.roll(low, shift, 1), pltpu.roll(high, shift, 1)
    return jnp.where(lane == at, high, low), jnp.where(lane == at, low, high)


def dice_kernel(prob_ref, label_ref, sums_ref, edge_ref, numer_ref, denom_ref):
    padded = prob_ref.shape[1]
    rows = prob_ref.shape[0] - 4
    groups = [(at, min(16, padded - at)) for at in range(0, padded, 16)]

    def tiles_of(ref, row, group):
        at, size = group
        return [ref[row, at : at + size, i * TILE : (i + 1) * TILE] for i in range(2)]

    def lanes(size):
        return lax.broadcasted_iota(jnp.int32, (size, TILE), 1)

    @pl.loop(0, rows + 2)
    def _(row):
        for group in groups:
            at, size = group
            centre = tiles_of(prob_ref, row + 1, group)
            before, after = tiles_of(prob_ref, row, group), tiles_of(prob_ref, row + 2, group)
            left, right = turn(centre, True, lanes(size)), turn(centre, False, lanes(size))
            for i in range(2):
                low = jnp.minimum(
                    jnp.minimum(before[i], after[i]), jnp.minimum(left[i], right[i])
                )
                edge_ref[row, at : at + size, i * TILE : (i + 1) * TILE] = centre[
                    i
                ] - jnp.minimum(centre[i], low)

    numer_ref[...] = jnp.zeros_like(numer_ref)
    denom_ref[...] = jnp.zeros_like(denom_ref)

    @pl.loop(0, rows)
    def _(row):
        def labels_of(at):
            line = label_ref[pl.ds(at, 1), :]
            return [line[:, i * TILE : (i + 1) * TILE] for i in range(2)]

        middle = labels_of(row + 1)
        line = lanes(1)
        near = (labels_of(row), labels_of(row + 2), turn(middle, True, line), turn(middle, False, line))
        near = [[other[i].astype(jnp.bfloat16) for i in range(2)] for other in near]
        middle = [middle[i].astype(jnp.bfloat16) for i in range(2)]
        for group in groups:
            at, size = group
            klass = (
                lax.broadcasted_iota(jnp.int32, (size, TILE), 0) + (1 + at)
            ).astype(jnp.float32).astype(jnp.bfloat16)
            lane = lanes(size)
            zero = jnp.zeros((size, TILE), jnp.bfloat16)
            centre = tiles_of(edge_ref, row + 1, group)
            before, after = tiles_of(edge_ref, row, group), tiles_of(edge_ref, row + 2, group)
            left, right = turn(centre, True, lane), turn(centre, False, lane)
            numer = numer_ref[at : at + size, :]
            denom = denom_ref[at : at + size, :]
            for i in range(2):
                wide = jnp.maximum(
                    jnp.maximum(centre[i], jnp.maximum(before[i], after[i])),
                    jnp.maximum(left[i], right[i]),
                )
                here = middle[i] == klass
                about = here
                for other in near:
                    about = about | (other[i] == klass)
                value = jnp.where(about, centre[i], zero).astype(jnp.float32)
                value = value + jnp.where(here, wide, zero).astype(jnp.float32)
                total = centre[i].astype(jnp.float32) + jnp.where(here, zero + 1, zero).astype(
                    jnp.float32
                )
                if i == 1:
                    value = jnp.where(lane < 64, value, 0.0)
                    total = jnp.where(lane < 64, total, 0.0)
                numer = numer + value
                denom = denom + total
            numer_ref[at : at + size, :] = numer
            denom_ref[at : at + size, :] = denom

    sums_ref[0] = jnp.broadcast_to(
        jnp.sum(numer_ref[...], axis=1, keepdims=True), (padded, TILE)
    )
    sums_ref[1] = jnp.broadcast_to(
        jnp.sum(denom_ref[...], axis=1, keepdims=True), (padded, TILE)
    )


def dice_of(prob, label):
    rows, padded, _ = prob.shape
    whole = pl.BlockSpec(memory_space=pltpu.VMEM)
    return pl.pallas_call(
        dice_kernel,
        out_shape=jax.ShapeDtypeStruct((2, padded, TILE), jnp.float32),
        in_specs=[whole] * 2,
        out_specs=whole,
        scratch_shapes=[
            pltpu.VMEM((rows - 2, padded, RING), jnp.bfloat16),
            pltpu.VMEM((padded, TILE), jnp.float32),
            pltpu.VMEM((padded, TILE), jnp.float32),
        ],
        compiler_params=pltpu.CompilerParams(vmem_limit_bytes=VMEM_LIMIT),
        cost_estimate=pl.CostEstimate(
            flops=prob.size * 30, bytes_accessed=prob.size * 2, transcendentals=0
        ),
        name="dice",
    )(prob, label)


def emit_kernel(chunks, *refs):
    prob_refs = refs[: len(chunks)]
    out_ref, turned_ref, sems = refs[-3:]
    _, span_y, classes = out_ref.shape
    span_x = out_ref.shape[0]

    copies = []
    base = 0
    for prob_ref, (first, rows) in zip(prob_refs, chunks):
        for i, at in enumerate((first, span_x - first - rows)):

            @pl.loop(0, rows)
            def _(index):
                for j in range(2):
                    block = prob_ref[i * rows + index, :, j * TILE : (j + 1) * TILE]
                    block = jnp.transpose(block.astype(jnp.float32), (1, 0))
                    stop = min((j + 1) * TILE, span_y)
                    turned_ref[base + index, j * TILE : stop, :] = block[
                        : stop - j * TILE, :classes
                    ].astype(jnp.bfloat16)

            copy = pltpu.make_async_copy(
                turned_ref.at[pl.ds(base, rows)], out_ref.at[pl.ds(at, rows)], sems.at[len(copies)]
            )
            copy.start()
            copies.append(copy)
            base += rows
    for copy in copies:
        copy.wait()


def emit(probs, chunks, shape, *before):
    anywhere = pl.BlockSpec(memory_space=pl.ANY)
    rows = sum(prob.shape[0] for prob in probs)
    size = sum(prob.size for prob in probs)
    return pl.pallas_call(
        functools.partial(emit_kernel, chunks),
        out_shape=jax.ShapeDtypeStruct(shape, probs[0].dtype),
        in_specs=[pl.BlockSpec(memory_space=pltpu.VMEM)] * len(probs) + [anywhere] * len(before),
        out_specs=anywhere,
        input_output_aliases={len(probs): 0} if before else {},
        scratch_shapes=[
            pltpu.VMEM((rows,) + shape[1:], probs[0].dtype),
            pltpu.SemaphoreType.DMA((2 * len(chunks),)),
        ],
        compiler_params=pltpu.CompilerParams(vmem_limit_bytes=VMEM_LIMIT),
        cost_estimate=pl.CostEstimate(
            flops=size * 4, bytes_accessed=size * 4, transcendentals=0
        ),
        name="emit",
    )(*probs, *before)


def shifted(block, axis, by):
    devices = lax.axis_size(axis)
    pairs = [(i, i + by) for i in range(devices) if 0 <= i + by < devices]
    return lax.ppermute(block, axis, pairs)


def gauss_line():
    position = jnp.arange(PATCH, dtype=jnp.float32) - (PATCH - 1) / 2.0
    sigma = 0.125 * PATCH
    return position * position / (2.0 * sigma * sigma)


def gauss_table():
    line = gauss_line()
    table = jnp.exp(-(line[:, None] + line[None, :]))
    return jnp.pad(table, ((0, QUAD), (0, TILE - PATCH)))


def three_parts(values):
    high = values.astype(jnp.bfloat16)
    rest = values - high.astype(jnp.float32)
    middle = rest.astype(jnp.bfloat16)
    low = (rest - middle.astype(jnp.float32)).astype(jnp.bfloat16)
    return jnp.stack([high, middle, low], axis=1)


def head_matrix(out_weight, out_bias):
    classes, feat = out_weight.shape
    matrix = jnp.concatenate(
        [out_weight, three_parts(out_bias), jnp.zeros((classes, 13), jnp.bfloat16)], axis=1
    )
    return jnp.concatenate([matrix, matrix[-2:]], axis=0)


def ring_of(plane):
    gap = jnp.zeros((plane.shape[0], RING - plane.shape[1]), plane.dtype)
    return jnp.concatenate([plane[:, 2:], gap, plane[:, :2]], axis=1)


def rows_of(plane, first, rows):
    span = plane.shape[0]
    return jnp.concatenate(
        [plane[first : first + rows], plane[span - first - rows : span - first]], axis=0
    )


def on_device(features, patch_ids, patch_count, labels, mlp_weight, mlp_bias, out_weight, out_bias):
    wide, narrow = lax.axis_size("wide"), lax.axis_size("narrow")
    here_wide, here_narrow = lax.axis_index("wide"), lax.axis_index("narrow")
    feat = features.shape[3]
    slots = features.shape[2]
    classes = out_weight.shape[0]
    span_x, span_y = labels.shape
    rows_q = ROWS * narrow
    feats = features[0, 0]

    slot_ids = jnp.arange(slots, dtype=jnp.int32)
    halves = jnp.arange(2, dtype=jnp.int32)
    columns = jnp.arange(2 * wide, dtype=jnp.int32)
    listed = slot_ids < patch_count[0, 0]
    column_of = patch_ids[0, 0][:, None] // rows_q + halves[None, :]
    hit = listed[:, None, None] & (column_of[:, :, None] == columns[None, None, :])
    pick = jnp.max(
        jnp.where(hit, (2 * slot_ids[:, None] + halves[None, :])[:, :, None], -1), axis=(0, 1)
    )

    def exchange(chunk, *after):
        payload = pack(feats, pick, *CHUNKS[chunk], *after)
        shape = payload.shape
        payload = payload.reshape((wide, 2) + shape[1:])
        return lax.all_to_all(payload, "wide", 0, 0, tiled=True).reshape(shape)

    received = [exchange(0), exchange(1)]

    kind = (patch_ids[0, 0] % rows_q - ROWS * here_narrow)[:, None] * 2 + halves[None, :]
    tag = jnp.max(jnp.where(hit, kind[:, :, None], -1), axis=(0, 1)).reshape(wide, 2)
    marked = labels + 1
    others = jnp.arange(wide, dtype=jnp.int32)[:, None]
    edges = jnp.where(others == here_wide + 1, marked[span_x - 2 :].reshape(1, -1), 0)
    edges = jnp.where(others == here_wide - 1, marked[:2].reshape(1, -1), edges)
    notes = lax.all_to_all(
        jnp.concatenate([tag, edges], axis=1), "wide", 0, 0, tiled=True
    )
    tag = notes[:, :2].reshape(-1)

    def rows_from(device):
        return jnp.sum(jnp.where(others == device, notes[:, 2:], 0), axis=0).reshape(2, span_y)

    label_wide = jnp.concatenate(
        [rows_from(here_wide - 1), marked, rows_from(here_wide + 1)], axis=0
    )
    valid = tag >= 0
    order = jnp.cumsum(valid.astype(jnp.int32)) - 1
    code = jnp.where(valid, columns * 8 + tag, 0)
    place = valid[:, None] & (order[:, None] == columns[None, :])
    codes = jnp.concatenate(
        [
            jnp.sum(jnp.where(place, code[:, None], 0), axis=0),
            jnp.sum(valid.astype(jnp.int32))[None],
        ]
    )

    table = gauss_table()
    square = table[:PATCH, :PATCH].reshape(2, QUAD, PATCH)
    kinds = jnp.arange(2 * ROWS, dtype=jnp.int32)
    counts = jnp.sum((tag.reshape(wide, 2, 1) == kinds).astype(jnp.float32), axis=0)

    def beside(columns, by):
        block = jnp.concatenate(
            [columns.astype(jnp.float32), counts.reshape(2 * ROWS, 2)], axis=0
        )
        return shifted(block, "narrow", by)

    def parts_of(block):
        return block[:-2 * ROWS].astype(jnp.int32), block[-2 * ROWS :].reshape(2, 2 * ROWS)

    blocks = beside(label_wide[:, span_y - 2 :], 1), beside(label_wide[:, :2], -1)
    head_weight = head_matrix(out_weight, out_bias)
    bias_tile = jnp.broadcast_to(mlp_bias[:, None], (feat, TILE))

    def head_at(chunk):
        return head_of(
            received[chunk], codes, mlp_weight, bias_tile, head_weight, table, *CHUNKS[chunk], classes
        )

    heads = []
    for chunk in range(len(CHUNKS) - 1):
        heads.append(head_at(chunk))
        if chunk + 2 < len(CHUNKS):
            received.append(exchange(chunk + 2, heads[chunk][2]))
    _, low_block, high_block = lax.optimization_barrier((heads[1][2],) + blocks)
    label_low, counts_low = parts_of(low_block)
    label_high, counts_high = parts_of(high_block)

    def plane_of(counts, row):
        pairs = counts.reshape(2, ROWS, 2)[:, row, :, None, None]
        return jnp.sum(pairs * square[None], axis=1).reshape(span_x, PATCH)

    norm = sum(
        jnp.pad(plane_of(counts, i), ((0, 0), (QUAD * i, QUAD * (ROWS - 1 - i))))
        for i in range(ROWS)
    )
    came = plane_of(counts_low, 3)
    norm = jnp.concatenate(
        [
            came[:, 46:48] + plane_of(counts_low, 2)[:, 94:96],
            norm[:, :QUAD] + came[:, 48:],
            norm[:, QUAD:span_y],
            norm[:, span_y : span_y + 2] + plane_of(counts_high, 0)[:, :2],
        ],
        axis=1,
    )
    across = ROWS * QUAD * here_narrow - 2 + jnp.arange(span_y + 4, dtype=jnp.int32)
    inside = (across >= 0) & (across < narrow * span_y)
    inverse = ring_of(jnp.where(inside[None, :], 1.0 / (norm + 0.001), 0.0))

    label_wide = jnp.concatenate([label_low, label_wide, label_high], axis=1)
    centre = label_wide[1:-1, 1:-1]
    same = (
        (label_wide[:-2, 1:-1] == centre)
        & (label_wide[2:, 1:-1] == centre)
        & (label_wide[1:-1, :-2] == centre)
        & (label_wide[1:-1, 2:] == centre)
    )
    boundary = jnp.where(same, 0, centre)
    boundary = ring_of(jnp.pad(boundary, ((0, 0), (1, 1))))

    probs = []
    for chunk, (first, rows) in enumerate(CHUNKS):
        own, up, down = heads[chunk] if chunk + 1 < len(CHUNKS) else head_at(chunk)
        up = shifted(up, "narrow", 1)
        down = shifted(down, "narrow", -1)
        prob = blend_of(own, up, down, rows_of(inverse, first, rows))
        probs.append(prob)
    edge_rows = CHUNKS[0][1]
    before = shifted(probs[0][2 * edge_rows - 2 :], "wide", 1)
    after = shifted(probs[0][:2], "wide", -1)
    last, last_rows = CHUNKS[-1]
    lows = [prob[:rows] for prob, (_, rows) in zip(probs, CHUNKS)]
    highs = [prob[rows:] for prob, (_, rows) in zip(probs, CHUNKS)]
    low = jnp.concatenate([before] + lows[:-1], axis=0)
    high = jnp.concatenate(highs[:-1][::-1] + [after], axis=0)
    middle = jnp.concatenate([lows[-2][-4:], probs[-1], highs[-2][:4]], axis=0)
    sums = (
        dice_of(low, boundary[:last])
        + dice_of(high, boundary[span_x - last + 2 :])
        + dice_of(middle, boundary[last - 2 : span_x - last + 4])
    )[:, :, 0]
    shape = (span_x, span_y, classes)
    blended = emit(probs[:-2], CHUNKS[:-2], shape)
    blended = emit(probs[-2:], CHUNKS[-2:], shape, blended)
    whole = jnp.broadcast_to(sums[None], (wide * narrow,) + sums.shape)
    whole = jnp.sum(lax.all_to_all(whole, ("wide", "narrow"), 0, 0, tiled=True), axis=0)
    dice = ((whole[0] + 1.0) / (whole[1] + 1.0))[:classes]
    slab_sums = (sums[:, :classes] / jnp.float32(span_x)).reshape(1, 1, 2, classes)
    return (blended.transpose(2, 0, 1), dice, slab_sums)


def solution(mesh):
    return jax.shard_map(
        on_device,
        mesh=mesh,
        in_specs=(
            P("wide", "narrow", None, None, None),
            P("wide", "narrow", None),
            P("wide", "narrow"),
            P("wide", "narrow"),
            P(),
            P(),
            P(),
            P(),
        ),
        out_specs=(P(None, "wide", "narrow"), P(), P("wide", "narrow", None, None)),
        check_vma=False,
    )
```

```python
import functools

import jax
import jax.numpy as jnp
from jax import lax
from jax.experimental import pallas as pl
from jax.experimental.pallas import tpu as pltpu
from jax.sharding import PartitionSpec as P

PATCH = 96
QUAD = 48
TILE = 128
RING = 256
ROWS = 4
CHUNKS = ((0, 12), (12, 20), (32, 16))
VMEM_LIMIT = 50 * 1024 * 1024


def pack_kernel(first, rows, pick_ref, feats_ref, *refs):
    out_ref, sems = refs[-2:]
    width = rows * PATCH

    def copy_of(column):
        source = pick_ref[column]
        start = first if column % 2 == 0 else QUAD - first - rows
        lane = pl.multiple_of((source % 2) * (QUAD * PATCH) + start * PATCH, TILE)
        return pltpu.make_async_copy(
            feats_ref.at[source // 2, :, pl.ds(lane, width)], out_ref.at[column], sems.at[column]
        )

    columns = out_ref.shape[0]
    for column in range(columns):

        @pl.when(pick_ref[column] >= 0)
        def _():
            copy_of(column).start()

    for column in range(columns):

        @pl.when(pick_ref[column] >= 0)
        def _():
            copy_of(column).wait()


def pack(feats, pick, first, rows, *after):
    columns = pick.shape[0]
    width = rows * PATCH
    return pl.pallas_call(
        functools.partial(pack_kernel, first, rows),
        out_shape=jax.ShapeDtypeStruct((columns, feats.shape[1], width), feats.dtype),
        in_specs=[pl.BlockSpec(memory_space=pltpu.SMEM)]
        + [pl.BlockSpec(memory_space=pl.ANY)] * (1 + len(after)),
        out_specs=pl.BlockSpec(memory_space=pltpu.VMEM),
        scratch_shapes=[pltpu.SemaphoreType.DMA((columns,))],
        compiler_params=pltpu.CompilerParams(vmem_limit_bytes=VMEM_LIMIT),
        cost_estimate=pl.CostEstimate(
            flops=0, bytes_accessed=columns * width * feats.shape[1] * 4, transcendentals=0
        ),
        name="pack",
    )(pick, feats, *after)


def head_kernel(
    first, rows, classes, code_ref, recv_ref, mlp_ref, bias_ref, head_ref, gauss_ref,
    own_ref, up_ref, down_ref, acc_ref, edge_ref, act0_ref, act1_ref, logit0_ref, logit1_ref,
    half_ref, half_sems, merged_ref, merged_sems,
):
    feat = recv_ref.shape[1]
    padded = head_ref.shape[0]
    lane = lax.broadcasted_iota(jnp.int32, (padded, TILE), 1)
    real = lax.broadcasted_iota(jnp.int32, (padded, TILE), 0) < classes
    mlp = mlp_ref[...]
    head = head_ref[...]
    count = code_ref[code_ref.shape[0] - 1]

    def half_copy(item):
        return pltpu.make_async_copy(
            recv_ref.at[code_ref[item] // 8], half_ref.at[item], half_sems.at[item]
        )

    def arrived(item):
        @pl.when(item < count)
        def _():
            half_copy(item).wait()

    @pl.loop(0, count)
    def _(item):
        half_copy(item).start()

    for act_ref in (act0_ref, act1_ref):
        act_ref[feat:, :] = jnp.ones((act_ref.shape[0] - feat, rows * PATCH), jnp.bfloat16)

    @pl.loop(0, ROWS)
    def _(which):
        @pl.loop(0, rows // 2)
        def _(group):
            acc_ref[which, group] = jnp.zeros((padded, 4 * PATCH), jnp.float32)

    edge_ref[...] = jnp.zeros_like(edge_ref)

    def raise_logits(item, act_ref, logit_ref):
        flat = half_ref[jnp.minimum(item, count - 1)]
        hidden = jnp.dot(mlp, flat, preferred_element_type=jnp.float32)
        for i in range(rows * PATCH // TILE):
            part = slice(i * TILE, (i + 1) * TILE)
            act_ref[0:feat, part] = (
                flat[:, part].astype(jnp.float32)
                + jnp.maximum(hidden[:, part] + bias_ref[...], 0.0)
            ).astype(jnp.bfloat16)
        logit_ref[...] = jnp.dot(head, act_ref[...], preferred_element_type=jnp.float32)

    def add_up(item, logit_ref):
        code = code_ref[jnp.minimum(item, count - 1)]
        which = (code // 2) % 4
        side = (code // 8) % 2
        start = (code % 2) * QUAD + jnp.where(side == 0, first, QUAD - first - rows)
        start = jnp.where(item < count, start, PATCH)
        for i in range(rows * PATCH // TILE):
            part = logit_ref[:, i * TILE : (i + 1) * TILE]
            top = jnp.max(part, axis=0, keepdims=True)
            raised = jnp.where(real, jnp.exp(part - top), 0.0)
            group, lanes = i // 3, slice(i % 3 * TILE, (i % 3 + 1) * TILE)
            scale = gauss_ref[start // 4 + group, i % 3] / jnp.sum(
                raised, axis=0, keepdims=True
            )
            acc_ref[which, side * (rows // 4) + group, :, lanes] += (
                (raised * scale).astype(jnp.bfloat16).astype(jnp.float32)
            )

    @pl.when(count > 0)
    def _():
        arrived(0)
        raise_logits(0, act0_ref, logit0_ref)

        @pl.loop(0, (count + 1) // 2)
        def _(pair):
            arrived(2 * pair + 1)
            arrived(2 * pair + 2)
            raise_logits(2 * pair + 1, act1_ref, logit1_ref)
            add_up(2 * pair, logit0_ref)
            raise_logits(2 * pair + 2, act0_ref, logit0_ref)
            add_up(2 * pair + 1, logit1_ref)

    def merged(group, i):
        low = jnp.zeros((padded, TILE), jnp.float32)
        high = jnp.zeros((padded, TILE), jnp.float32)
        for which in range(ROWS):
            for tile in range(3):
                first_y = max(0, tile * TILE - i * PATCH) + which * QUAD
                last_y = min(PATCH, (tile + 1) * TILE - i * PATCH) + which * QUAD
                if first_y >= last_y:
                    continue
                part = acc_ref[which, group, :, tile * TILE : (tile + 1) * TILE]
                shift = (which * QUAD - i * PATCH) % TILE
                if shift:
                    part = pltpu.roll(part, shift, 1)
                if first_y < TILE:
                    keep = (lane >= first_y) & (lane < last_y)
                    low = low + jnp.where(keep, part, 0.0)
                if last_y > TILE:
                    keep = (lane >= first_y - TILE) & (lane < last_y - TILE)
                    high = high + jnp.where(keep, part, 0.0)
        row = 4 * group + i
        merged_ref[row, :, 0:TILE] = low
        merged_ref[row, :, TILE:RING] = high
        edge_ref[...] = jnp.where(
            (lane == 2 * row) | (lane == 2 * row + 1), pltpu.roll(low, 2 * row, 1), edge_ref[...]
        )
        return high

    def own_copy(group):
        place = pl.ds(4 * group, 4)
        return pltpu.make_async_copy(
            merged_ref.at[place], own_ref.at[place], merged_sems.at[group]
        )

    @pl.loop(0, rows // 2)
    def _(group):
        for i in range(2):
            even = merged(group, 2 * i)
            odd = merged(group, 2 * i + 1)
            up_ref[2 * group + i] = jnp.where(
                lane < 64, pltpu.roll(even, 66, 1), pltpu.roll(odd, 2, 1)
            ).astype(jnp.bfloat16)
        own_copy(group).start()

    @pl.loop(0, rows // 2)
    def _(group):
        own_copy(group).wait()

    down_ref[...] = edge_ref[...].astype(jnp.bfloat16)


def head_of(recv, codes, mlp_weight, bias_tile, head_weight, gauss, first, rows, classes):
    padded = head_weight.shape[0]
    whole = pl.BlockSpec(memory_space=pltpu.VMEM)
    return pl.pallas_call(
        functools.partial(head_kernel, first, rows, classes),
        out_shape=(
            jax.ShapeDtypeStruct((2 * rows, padded, RING), jnp.float32),
            jax.ShapeDtypeStruct((rows, padded, TILE), jnp.bfloat16),
            jax.ShapeDtypeStruct((padded, TILE), jnp.bfloat16),
        ),
        in_specs=[
            pl.BlockSpec(memory_space=pltpu.SMEM), pl.BlockSpec(memory_space=pl.ANY)
        ]
        + [whole] * 4,
        out_specs=(pl.BlockSpec(memory_space=pl.ANY), whole, whole),
        scratch_shapes=[
            pltpu.VMEM((ROWS, rows // 2, padded, 4 * PATCH), jnp.float32),
            pltpu.VMEM((padded, TILE), jnp.float32),
            pltpu.VMEM((head_weight.shape[1], rows * PATCH), jnp.bfloat16),
            pltpu.VMEM((head_weight.shape[1], rows * PATCH), jnp.bfloat16),
            pltpu.VMEM((padded, rows * PATCH), jnp.float32),
            pltpu.VMEM((padded, rows * PATCH), jnp.float32),
            pltpu.VMEM(recv.shape, recv.dtype),
            pltpu.SemaphoreType.DMA(recv.shape[:1]),
            pltpu.VMEM((2 * rows, padded, RING), jnp.float32),
            pltpu.SemaphoreType.DMA((rows // 2,)),
        ],
        compiler_params=pltpu.CompilerParams(vmem_limit_bytes=VMEM_LIMIT),
        cost_estimate=pl.CostEstimate(
            flops=rows * 900_000_000 // 48, bytes_accessed=rows * 25_000_000 // 48,
            transcendentals=rows * 12_000_000 // 48,
        ),
        name="head",
    )(codes, recv, mlp_weight, bias_tile, head_weight, gauss)


def blend_kernel(own_ref, up_ref, down_ref, inv_ref, prob_ref):
    rows, padded, _ = own_ref.shape
    lane = lax.broadcasted_iota(jnp.int32, (padded, TILE), 1)
    first = lax.broadcasted_iota(jnp.int32, (padded, TILE), 0) == 0
    extra = jnp.where(first, 0.001, 0.0)
    down = down_ref[...].astype(jnp.float32)
    base = pl.program_id(0) * rows

    for row in range(rows):
        came = up_ref[row // 2].astype(jnp.float32)
        came = pltpu.roll(came, 126 if row % 2 == 0 else 62, 1)
        low = own_ref[row, :, 0:TILE] + jnp.where(lane < 48, came, 0.0)
        high = own_ref[row, :, TILE:RING] + jnp.where(lane >= 126, came, 0.0)
        after = pltpu.roll(down, lax.rem(192 - 2 * (base + row), TILE), 1)
        high = high + jnp.where((lane == 64) | (lane == 65), after, 0.0)
        scale = inv_ref[pl.ds(base + row, 1), :]
        prob_ref[row, :, 0:TILE] = ((low + extra) * scale[:, 0:TILE]).astype(jnp.bfloat16)
        prob_ref[row, :, TILE:RING] = ((high + extra) * scale[:, TILE:RING]).astype(jnp.bfloat16)


def blend_of(own, up, down, inv):
    rows, padded, _ = own.shape
    whole = pl.BlockSpec(memory_space=pltpu.VMEM)
    step = 8
    return pl.pallas_call(
        blend_kernel,
        grid=(rows // step,),
        out_shape=jax.ShapeDtypeStruct(own.shape, jnp.bfloat16),
        in_specs=[
            pl.BlockSpec((step, padded, RING), lambda i: (i, 0, 0)),
            pl.BlockSpec((step // 2, padded, TILE), lambda i: (i, 0, 0)),
            whole,
            whole,
        ],
        out_specs=pl.BlockSpec((step, padded, RING), lambda i: (i, 0, 0)),
        compiler_params=pltpu.CompilerParams(vmem_limit_bytes=VMEM_LIMIT),
        cost_estimate=pl.CostEstimate(
            flops=own.size * 4, bytes_accessed=own.size * 7, transcendentals=0
        ),
        name="blend",
    )(own, up, down, inv)


def turn(tiles, forward, lane):
    low, high = tiles
    shift, at = (1, 0) if forward else (TILE - 1, TILE - 1)
    low, high = pltpu.roll(low, shift, 1), pltpu.roll(high, shift, 1)
    return jnp.where(lane == at, high, low), jnp.where(lane == at, low, high)


def dice_kernel(prob_ref, label_ref, sums_ref, edge_ref, numer_ref, denom_ref):
    padded = prob_ref.shape[1]
    rows = prob_ref.shape[0] - 4
    groups = [(at, min(16, padded - at)) for at in range(0, padded, 16)]

    def tiles_of(ref, row, group):
        at, size = group
        return [ref[row, at : at + size, i * TILE : (i + 1) * TILE] for i in range(2)]

    def lanes(size):
        return lax.broadcasted_iota(jnp.int32, (size, TILE), 1)

    @pl.loop(0, rows + 2)
    def _(row):
        for group in groups:
            at, size = group
            centre = tiles_of(prob_ref, row + 1, group)
            before, after = tiles_of(prob_ref, row, group), tiles_of(prob_ref, row + 2, group)
            left, right = turn(centre, True, lanes(size)), turn(centre, False, lanes(size))
            for i in range(2):
                low = jnp.minimum(
                    jnp.minimum(before[i], after[i]), jnp.minimum(left[i], right[i])
                )
                edge_ref[row, at : at + size, i * TILE : (i + 1) * TILE] = centre[
                    i
                ] - jnp.minimum(centre[i], low)

    numer_ref[...] = jnp.zeros_like(numer_ref)
    denom_ref[...] = jnp.zeros_like(denom_ref)

    @pl.loop(0, rows)
    def _(row):
        def labels_of(at):
            line = label_ref[pl.ds(at, 1), :]
            return [line[:, i * TILE : (i + 1) * TILE] for i in range(2)]

        middle = labels_of(row + 1)
        line = lanes(1)
        near = (labels_of(row), labels_of(row + 2), turn(middle, True, line), turn(middle, False, line))
        near = [[other[i].astype(jnp.bfloat16) for i in range(2)] for other in near]
        middle = [middle[i].astype(jnp.bfloat16) for i in range(2)]
        for group in groups:
            at, size = group
            klass = (
                lax.broadcasted_iota(jnp.int32, (size, TILE), 0) + (1 + at)
            ).astype(jnp.float32).astype(jnp.bfloat16)
            lane = lanes(size)
            zero = jnp.zeros((size, TILE), jnp.bfloat16)
            centre = tiles_of(edge_ref, row + 1, group)
            before, after = tiles_of(edge_ref, row, group), tiles_of(edge_ref, row + 2, group)
            left, right = turn(centre, True, lane), turn(centre, False, lane)
            numer = numer_ref[at : at + size, :]
            denom = denom_ref[at : at + size, :]
            for i in range(2):
                wide = jnp.maximum(
                    jnp.maximum(centre[i], jnp.maximum(before[i], after[i])),
                    jnp.maximum(left[i], right[i]),
                )
                here = middle[i] == klass
                about = here
                for other in near:
                    about = about | (other[i] == klass)
                value = jnp.where(about, centre[i], zero).astype(jnp.float32)
                value = value + jnp.where(here, wide, zero).astype(jnp.float32)
                total = centre[i].astype(jnp.float32) + jnp.where(here, zero + 1, zero).astype(
                    jnp.float32
                )
                if i == 1:
                    value = jnp.where(lane < 64, value, 0.0)
                    total = jnp.where(lane < 64, total, 0.0)
                numer = numer + value
                denom = denom + total
            numer_ref[at : at + size, :] = numer
            denom_ref[at : at + size, :] = denom

    sums_ref[0] = jnp.broadcast_to(
        jnp.sum(numer_ref[...], axis=1, keepdims=True), (padded, TILE)
    )
    sums_ref[1] = jnp.broadcast_to(
        jnp.sum(denom_ref[...], axis=1, keepdims=True), (padded, TILE)
    )


def dice_of(prob, label):
    rows, padded, _ = prob.shape
    whole = pl.BlockSpec(memory_space=pltpu.VMEM)
    return pl.pallas_call(
        dice_kernel,
        out_shape=jax.ShapeDtypeStruct((2, padded, TILE), jnp.float32),
        in_specs=[whole] * 2,
        out_specs=whole,
        scratch_shapes=[
            pltpu.VMEM((rows - 2, padded, RING), jnp.bfloat16),
            pltpu.VMEM((padded, TILE), jnp.float32),
            pltpu.VMEM((padded, TILE), jnp.float32),
        ],
        compiler_params=pltpu.CompilerParams(vmem_limit_bytes=VMEM_LIMIT),
        cost_estimate=pl.CostEstimate(
            flops=prob.size * 30, bytes_accessed=prob.size * 2, transcendentals=0
        ),
        name="dice",
    )(prob, label)


def emit_kernel(chunks, *refs):
    prob_refs = refs[: len(chunks)]
    out_ref, turned_ref, sems = refs[-3:]
    _, span_y, classes = out_ref.shape
    span_x = out_ref.shape[0]

    copies = []
    base = 0
    for prob_ref, (first, rows) in zip(prob_refs, chunks):
        for i, at in enumerate((first, span_x - first - rows)):

            @pl.loop(0, rows)
            def _(index):
                for j in range(2):
                    block = prob_ref[i * rows + index, :, j * TILE : (j + 1) * TILE]
                    block = jnp.transpose(block.astype(jnp.float32), (1, 0))
                    stop = min((j + 1) * TILE, span_y)
                    turned_ref[base + index, j * TILE : stop, :] = block[
                        : stop - j * TILE, :classes
                    ].astype(jnp.bfloat16)

            copy = pltpu.make_async_copy(
                turned_ref.at[pl.ds(base, rows)], out_ref.at[pl.ds(at, rows)], sems.at[len(copies)]
            )
            copy.start()
            copies.append(copy)
            base += rows
    for copy in copies:
        copy.wait()


def emit(probs, chunks, shape, *before):
    anywhere = pl.BlockSpec(memory_space=pl.ANY)
    rows = sum(prob.shape[0] for prob in probs)
    size = sum(prob.size for prob in probs)
    return pl.pallas_call(
        functools.partial(emit_kernel, chunks),
        out_shape=jax.ShapeDtypeStruct(shape, probs[0].dtype),
        in_specs=[pl.BlockSpec(memory_space=pltpu.VMEM)] * len(probs) + [anywhere] * len(before),
        out_specs=anywhere,
        input_output_aliases={len(probs): 0} if before else {},
        scratch_shapes=[
            pltpu.VMEM((rows,) + shape[1:], probs[0].dtype),
            pltpu.SemaphoreType.DMA((2 * len(chunks),)),
        ],
        compiler_params=pltpu.CompilerParams(vmem_limit_bytes=VMEM_LIMIT),
        cost_estimate=pl.CostEstimate(
            flops=size * 4, bytes_accessed=size * 4, transcendentals=0
        ),
        name="emit",
    )(*probs, *before)


def shifted(block, axis, by):
    devices = lax.axis_size(axis)
    pairs = [(i, i + by) for i in range(devices) if 0 <= i + by < devices]
    return lax.ppermute(block, axis, pairs)


def gauss_line():
    position = jnp.arange(PATCH, dtype=jnp.float32) - (PATCH - 1) / 2.0
    sigma = 0.125 * PATCH
    return position * position / (2.0 * sigma * sigma)


def gauss_table():
    line = gauss_line()
    table = jnp.exp(-(line[:, None] + line[None, :]))
    return jnp.pad(table, ((0, QUAD), (0, TILE - PATCH)))


def three_parts(values):
    high = values.astype(jnp.bfloat16)
    rest = values - high.astype(jnp.float32)
    middle = rest.astype(jnp.bfloat16)
    low = (rest - middle.astype(jnp.float32)).astype(jnp.bfloat16)
    return jnp.stack([high, middle, low], axis=1)


def head_matrix(out_weight, out_bias):
    classes, feat = out_weight.shape
    matrix = jnp.concatenate(
        [out_weight, three_parts(out_bias), jnp.zeros((classes, 13), jnp.bfloat16)], axis=1
    )
    return jnp.concatenate([matrix, matrix[-2:]], axis=0)


def ring_of(plane):
    gap = jnp.zeros((plane.shape[0], RING - plane.shape[1]), plane.dtype)
    return jnp.concatenate([plane[:, 2:], gap, plane[:, :2]], axis=1)


def rows_of(plane, first, rows):
    span = plane.shape[0]
    return jnp.concatenate(
        [plane[first : first + rows], plane[span - first - rows : span - first]], axis=0
    )


def on_device(features, patch_ids, patch_count, labels, mlp_weight, mlp_bias, out_weight, out_bias):
    wide, narrow = lax.axis_size("wide"), lax.axis_size("narrow")
    here_wide, here_narrow = lax.axis_index("wide"), lax.axis_index("narrow")
    feat = features.shape[3]
    slots = features.shape[2]
    classes = out_weight.shape[0]
    span_x, span_y = labels.shape
    rows_q = ROWS * narrow
    feats = features[0, 0]

    slot_ids = jnp.arange(slots, dtype=jnp.int32)
    halves = jnp.arange(2, dtype=jnp.int32)
    columns = jnp.arange(2 * wide, dtype=jnp.int32)
    listed = slot_ids < patch_count[0, 0]
    column_of = patch_ids[0, 0][:, None] // rows_q + halves[None, :]
    hit = listed[:, None, None] & (column_of[:, :, None] == columns[None, None, :])
    pick = jnp.max(
        jnp.where(hit, (2 * slot_ids[:, None] + halves[None, :])[:, :, None], -1), axis=(0, 1)
    )

    def exchange(chunk, *after):
        payload = pack(feats, pick, *CHUNKS[chunk], *after)
        shape = payload.shape
        payload = payload.reshape((wide, 2) + shape[1:])
        return lax.all_to_all(payload, "wide", 0, 0, tiled=True).reshape(shape)

    received = [exchange(0), exchange(1)]

    kind = (patch_ids[0, 0] % rows_q - ROWS * here_narrow)[:, None] * 2 + halves[None, :]
    tag = jnp.max(jnp.where(hit, kind[:, :, None], -1), axis=(0, 1)).reshape(wide, 2)
    marked = labels + 1
    others = jnp.arange(wide, dtype=jnp.int32)[:, None]
    edges = jnp.where(others == here_wide + 1, marked[span_x - 2 :].reshape(1, -1), 0)
    edges = jnp.where(others == here_wide - 1, marked[:2].reshape(1, -1), edges)
    notes = lax.all_to_all(
        jnp.concatenate([tag, edges], axis=1), "wide", 0, 0, tiled=True
    )
    tag = notes[:, :2].reshape(-1)

    def rows_from(device):
        return jnp.sum(jnp.where(others == device, notes[:, 2:], 0), axis=0).reshape(2, span_y)

    label_wide = jnp.concatenate(
        [rows_from(here_wide - 1), marked, rows_from(here_wide + 1)], axis=0
    )
    valid = tag >= 0
    order = jnp.cumsum(valid.astype(jnp.int32)) - 1
    code = jnp.where(valid, columns * 8 + tag, 0)
    place = valid[:, None] & (order[:, None] == columns[None, :])
    codes = jnp.concatenate(
        [
            jnp.sum(jnp.where(place, code[:, None], 0), axis=0),
            jnp.sum(valid.astype(jnp.int32))[None],
        ]
    )

    table = gauss_table()
    square = table[:PATCH, :PATCH].reshape(2, QUAD, PATCH)
    kinds = jnp.arange(2 * ROWS, dtype=jnp.int32)
    counts = jnp.sum((tag.reshape(wide, 2, 1) == kinds).astype(jnp.float32), axis=0)

    def beside(columns, by):
        block = jnp.concatenate(
            [columns.astype(jnp.float32), counts.reshape(2 * ROWS, 2)], axis=0
        )
        return shifted(block, "narrow", by)

    def parts_of(block):
        return block[:-2 * ROWS].astype(jnp.int32), block[-2 * ROWS :].reshape(2, 2 * ROWS)

    blocks = beside(label_wide[:, span_y - 2 :], 1), beside(label_wide[:, :2], -1)
    head_weight = head_matrix(out_weight, out_bias)
    bias_tile = jnp.broadcast_to(mlp_bias[:, None], (feat, TILE))

    def head_at(chunk):
        return head_of(
            received[chunk], codes, mlp_weight, bias_tile, head_weight,
            table[:, :PATCH].reshape(-1, 3, 1, TILE), *CHUNKS[chunk], classes
        )

    heads = []
    for chunk in range(len(CHUNKS) - 1):
        heads.append(head_at(chunk))
        if chunk + 2 < len(CHUNKS):
            received.append(exchange(chunk + 2, heads[chunk][2]))
    _, low_block, high_block = lax.optimization_barrier((heads[1][2],) + blocks)
    label_low, counts_low = parts_of(low_block)
    label_high, counts_high = parts_of(high_block)

    def plane_of(counts, row):
        pairs = counts.reshape(2, ROWS, 2)[:, row, :, None, None]
        return jnp.sum(pairs * square[None], axis=1).reshape(span_x, PATCH)

    norm = sum(
        jnp.pad(plane_of(counts, i), ((0, 0), (QUAD * i, QUAD * (ROWS - 1 - i))))
        for i in range(ROWS)
    )
    came = plane_of(counts_low, 3)
    norm = jnp.concatenate(
        [
            came[:, 46:48] + plane_of(counts_low, 2)[:, 94:96],
            norm[:, :QUAD] + came[:, 48:],
            norm[:, QUAD:span_y],
            norm[:, span_y : span_y + 2] + plane_of(counts_high, 0)[:, :2],
        ],
        axis=1,
    )
    across = ROWS * QUAD * here_narrow - 2 + jnp.arange(span_y + 4, dtype=jnp.int32)
    inside = (across >= 0) & (across < narrow * span_y)
    inverse = ring_of(jnp.where(inside[None, :], 1.0 / (norm + 0.001), 0.0))

    label_wide = jnp.concatenate([label_low, label_wide, label_high], axis=1)
    centre = label_wide[1:-1, 1:-1]
    same = (
        (label_wide[:-2, 1:-1] == centre)
        & (label_wide[2:, 1:-1] == centre)
        & (label_wide[1:-1, :-2] == centre)
        & (label_wide[1:-1, 2:] == centre)
    )
    boundary = jnp.where(same, 0, centre)
    boundary = ring_of(jnp.pad(boundary, ((0, 0), (1, 1))))

    probs = []
    for chunk, (first, rows) in enumerate(CHUNKS):
        own, up, down = heads[chunk] if chunk + 1 < len(CHUNKS) else head_at(chunk)
        up = shifted(up, "narrow", 1)
        down = shifted(down, "narrow", -1)
        prob = blend_of(own, up, down, rows_of(inverse, first, rows))
        probs.append(prob)
    edge_rows = CHUNKS[0][1]
    before = shifted(probs[0][2 * edge_rows - 2 :], "wide", 1)
    after = shifted(probs[0][:2], "wide", -1)
    last, last_rows = CHUNKS[-1]
    lows = [prob[:rows] for prob, (_, rows) in zip(probs, CHUNKS)]
    highs = [prob[rows:] for prob, (_, rows) in zip(probs, CHUNKS)]
    low = jnp.concatenate([before] + lows[:-1], axis=0)
    high = jnp.concatenate(highs[:-1][::-1] + [after], axis=0)
    middle = jnp.concatenate([lows[-2][-4:], probs[-1], highs[-2][:4]], axis=0)
    sums = (
        dice_of(low, boundary[:last])
        + dice_of(high, boundary[span_x - last + 2 :])
        + dice_of(middle, boundary[last - 2 : span_x - last + 4])
    )[:, :, 0]
    shape = (span_x, span_y, classes)
    blended = emit(probs[:-2], CHUNKS[:-2], shape)
    blended = emit(probs[-2:], CHUNKS[-2:], shape, blended)
    whole = jnp.broadcast_to(sums[None], (wide * narrow,) + sums.shape)
    whole = jnp.sum(lax.all_to_all(whole, ("wide", "narrow"), 0, 0, tiled=True), axis=0)
    dice = ((whole[0] + 1.0) / (whole[1] + 1.0))[:classes]
    slab_sums = (sums[:, :classes] / jnp.float32(span_x)).reshape(1, 1, 2, classes)
    return (blended.transpose(2, 0, 1), dice, slab_sums)


def solution(mesh):
    return jax.shard_map(
        on_device,
        mesh=mesh,
        in_specs=(
            P("wide", "narrow", None, None, None),
            P("wide", "narrow", None),
            P("wide", "narrow"),
            P("wide", "narrow"),
            P(),
            P(),
            P(),
            P(),
        ),
        out_specs=(P(None, "wide", "narrow"), P(), P("wide", "narrow", None, None)),
        check_vma=False,
    )
```

```python
import functools

import jax
import jax.numpy as jnp
from jax import lax
from jax.experimental import pallas as pl
from jax.experimental.pallas import tpu as pltpu
from jax.sharding import PartitionSpec as P

PATCH = 96
QUAD = 48
TILE = 128
RING = 256
ROWS = 4
CHUNKS = ((0, 12), (12, 20), (32, 16))
VMEM_LIMIT = 50 * 1024 * 1024


def pack_kernel(first, rows, pick_ref, feats_ref, *refs):
    out_ref, sems = refs[-2:]
    width = rows * PATCH

    def copy_of(column):
        source = pick_ref[column]
        start = first if column % 2 == 0 else QUAD - first - rows
        lane = pl.multiple_of((source % 2) * (QUAD * PATCH) + start * PATCH, TILE)
        return pltpu.make_async_copy(
            feats_ref.at[source // 2, :, pl.ds(lane, width)], out_ref.at[column], sems.at[column]
        )

    columns = out_ref.shape[0]
    for column in range(columns):

        @pl.when(pick_ref[column] >= 0)
        def _():
            copy_of(column).start()

    for column in range(columns):

        @pl.when(pick_ref[column] >= 0)
        def _():
            copy_of(column).wait()


def pack(feats, pick, first, rows, *after):
    columns = pick.shape[0]
    width = rows * PATCH
    return pl.pallas_call(
        functools.partial(pack_kernel, first, rows),
        out_shape=jax.ShapeDtypeStruct((columns, feats.shape[1], width), feats.dtype),
        in_specs=[pl.BlockSpec(memory_space=pltpu.SMEM)]
        + [pl.BlockSpec(memory_space=pl.ANY)] * (1 + len(after)),
        out_specs=pl.BlockSpec(memory_space=pltpu.VMEM),
        scratch_shapes=[pltpu.SemaphoreType.DMA((columns,))],
        compiler_params=pltpu.CompilerParams(vmem_limit_bytes=VMEM_LIMIT),
        cost_estimate=pl.CostEstimate(
            flops=0, bytes_accessed=columns * width * feats.shape[1] * 4, transcendentals=0
        ),
        name="pack",
    )(pick, feats, *after)


def head_kernel(
    first, rows, classes, code_ref, recv_ref, mlp_ref, bias_ref, head_ref, gauss_ref,
    own_ref, up_ref, down_ref, acc_ref, edge_ref, act0_ref, act1_ref, logit0_ref, logit1_ref,
    half_ref, half_sems, merged_ref, merged_sems,
):
    feat = recv_ref.shape[1]
    padded = head_ref.shape[0]
    lane = lax.broadcasted_iota(jnp.int32, (padded, TILE), 1)
    real = lax.broadcasted_iota(jnp.int32, (padded, TILE), 0) < classes
    mlp = mlp_ref[...]
    head = head_ref[...]
    count = code_ref[code_ref.shape[0] - 1]

    def half_copy(item):
        return pltpu.make_async_copy(
            recv_ref.at[code_ref[item] // 8], half_ref.at[item], half_sems.at[item]
        )

    def arrived(item):
        @pl.when(item < count)
        def _():
            half_copy(item).wait()

    @pl.loop(0, count)
    def _(item):
        half_copy(item).start()

    for act_ref in (act0_ref, act1_ref):
        act_ref[feat:, :] = jnp.ones((act_ref.shape[0] - feat, rows * PATCH), jnp.bfloat16)

    @pl.loop(0, ROWS)
    def _(which):
        @pl.loop(0, rows // 2)
        def _(group):
            acc_ref[which, group] = jnp.zeros((padded, 4 * PATCH), jnp.float32)

    edge_ref[...] = jnp.zeros_like(edge_ref)

    def raise_logits(item, act_ref, logit_ref):
        flat = half_ref[jnp.minimum(item, count - 1)]
        hidden = jnp.dot(mlp, flat, preferred_element_type=jnp.float32)
        for i in range(rows * PATCH // TILE):
            part = slice(i * TILE, (i + 1) * TILE)
            act_ref[0:feat, part] = (
                flat[:, part].astype(jnp.float32)
                + jnp.maximum(hidden[:, part] + bias_ref[...], 0.0)
            ).astype(jnp.bfloat16)
        logit_ref[...] = jnp.dot(head, act_ref[...], preferred_element_type=jnp.float32)

    def add_up(item, logit_ref):
        code = code_ref[jnp.minimum(item, count - 1)]
        which = (code // 2) % 4
        side = (code // 8) % 2
        start = (code % 2) * QUAD + jnp.where(side == 0, first, QUAD - first - rows)
        start = jnp.where(item < count, start, PATCH)
        for i in range(rows * PATCH // TILE):
            part = logit_ref[:, i * TILE : (i + 1) * TILE]
            top = jnp.max(part, axis=0, keepdims=True)
            raised = jnp.where(real, jnp.exp(part - top), 0.0)
            group, lanes = i // 3, slice(i % 3 * TILE, (i % 3 + 1) * TILE)
            scale = gauss_ref[start // 4 + group, i % 3] / jnp.sum(
                raised, axis=0, keepdims=True
            )
            acc_ref[which, side * (rows // 4) + group, :, lanes] += (
                (raised * scale).astype(jnp.bfloat16).astype(jnp.float32)
            )

    @pl.when(count > 0)
    def _():
        arrived(0)
        raise_logits(0, act0_ref, logit0_ref)

        @pl.loop(0, (count + 1) // 2)
        def _(pair):
            arrived(2 * pair + 1)
            arrived(2 * pair + 2)
            raise_logits(2 * pair + 1, act1_ref, logit1_ref)
            add_up(2 * pair, logit0_ref)
            raise_logits(2 * pair + 2, act0_ref, logit0_ref)
            add_up(2 * pair + 1, logit1_ref)

    def merged(group, i):
        low = jnp.zeros((padded, TILE), jnp.float32)
        high = jnp.zeros((padded, TILE), jnp.float32)
        for which in range(ROWS):
            for tile in range(3):
                first_y = max(0, tile * TILE - i * PATCH) + which * QUAD
                last_y = min(PATCH, (tile + 1) * TILE - i * PATCH) + which * QUAD
                if first_y >= last_y:
                    continue
                part = acc_ref[which, group, :, tile * TILE : (tile + 1) * TILE]
                shift = (which * QUAD - i * PATCH) % TILE
                if shift:
                    part = pltpu.roll(part, shift, 1)
                if first_y < TILE:
                    keep = (lane >= first_y) & (lane < last_y)
                    low = low + jnp.where(keep, part, 0.0)
                if last_y > TILE:
                    keep = (lane >= first_y - TILE) & (lane < last_y - TILE)
                    high = high + jnp.where(keep, part, 0.0)
        row = 4 * group + i
        merged_ref[row, :, 0:TILE] = low
        merged_ref[row, :, TILE:RING] = high
        edge_ref[...] = jnp.where(
            (lane == 2 * row) | (lane == 2 * row + 1), pltpu.roll(low, 2 * row, 1), edge_ref[...]
        )
        return high

    def own_copy(group):
        place = pl.ds(4 * group, 4)
        return pltpu.make_async_copy(
            merged_ref.at[place], own_ref.at[place], merged_sems.at[group]
        )

    @pl.loop(0, rows // 2)
    def _(group):
        for i in range(2):
            even = merged(group, 2 * i)
            odd = merged(group, 2 * i + 1)
            up_ref[2 * group + i] = jnp.where(
                lane < 64, pltpu.roll(even, 66, 1), pltpu.roll(odd, 2, 1)
            ).astype(jnp.bfloat16)
        own_copy(group).start()

    @pl.loop(0, rows // 2)
    def _(group):
        own_copy(group).wait()

    down_ref[...] = edge_ref[...].astype(jnp.bfloat16)


def head_of(recv, codes, mlp_weight, bias_tile, head_weight, gauss, first, rows, classes):
    padded = head_weight.shape[0]
    whole = pl.BlockSpec(memory_space=pltpu.VMEM)
    return pl.pallas_call(
        functools.partial(head_kernel, first, rows, classes),
        out_shape=(
            jax.ShapeDtypeStruct((2 * rows, padded, RING), jnp.float32),
            jax.ShapeDtypeStruct((rows, padded, TILE), jnp.bfloat16),
            jax.ShapeDtypeStruct((padded, TILE), jnp.bfloat16),
        ),
        in_specs=[
            pl.BlockSpec(memory_space=pltpu.SMEM), pl.BlockSpec(memory_space=pl.ANY)
        ]
        + [whole] * 4,
        out_specs=(pl.BlockSpec(memory_space=pl.ANY), whole, whole),
        scratch_shapes=[
            pltpu.VMEM((ROWS, rows // 2, padded, 4 * PATCH), jnp.float32),
            pltpu.VMEM((padded, TILE), jnp.float32),
            pltpu.VMEM((head_weight.shape[1], rows * PATCH), jnp.bfloat16),
            pltpu.VMEM((head_weight.shape[1], rows * PATCH), jnp.bfloat16),
            pltpu.VMEM((padded, rows * PATCH), jnp.float32),
            pltpu.VMEM((padded, rows * PATCH), jnp.float32),
            pltpu.VMEM(recv.shape, recv.dtype),
            pltpu.SemaphoreType.DMA(recv.shape[:1]),
            pltpu.VMEM((2 * rows, padded, RING), jnp.float32),
            pltpu.SemaphoreType.DMA((rows // 2,)),
        ],
        compiler_params=pltpu.CompilerParams(vmem_limit_bytes=VMEM_LIMIT),
        cost_estimate=pl.CostEstimate(
            flops=rows * 900_000_000 // 48, bytes_accessed=rows * 25_000_000 // 48,
            transcendentals=rows * 12_000_000 // 48,
        ),
        name="head",
    )(codes, recv, mlp_weight, bias_tile, head_weight, gauss)


def blend_kernel(own_ref, up_ref, down_ref, inv_ref, prob_ref):
    rows, padded, _ = own_ref.shape
    lane = lax.broadcasted_iota(jnp.int32, (padded, TILE), 1)
    first = lax.broadcasted_iota(jnp.int32, (padded, TILE), 0) == 0
    extra = jnp.where(first, 0.001, 0.0)
    down = down_ref[...].astype(jnp.float32)
    base = pl.program_id(0) * rows

    for row in range(rows):
        came = up_ref[row // 2].astype(jnp.float32)
        came = pltpu.roll(came, 126 if row % 2 == 0 else 62, 1)
        low = own_ref[row, :, 0:TILE] + jnp.where(lane < 48, came, 0.0)
        high = own_ref[row, :, TILE:RING] + jnp.where(lane >= 126, came, 0.0)
        after = pltpu.roll(down, lax.rem(192 - 2 * (base + row), TILE), 1)
        high = high + jnp.where((lane == 64) | (lane == 65), after, 0.0)
        scale = inv_ref[pl.ds(base + row, 1), :]
        prob_ref[row, :, 0:TILE] = ((low + extra) * scale[:, 0:TILE]).astype(jnp.bfloat16)
        prob_ref[row, :, TILE:RING] = ((high + extra) * scale[:, TILE:RING]).astype(jnp.bfloat16)


def blend_of(own, up, down, inv):
    rows, padded, _ = own.shape
    whole = pl.BlockSpec(memory_space=pltpu.VMEM)
    step = 8
    return pl.pallas_call(
        blend_kernel,
        grid=(rows // step,),
        out_shape=jax.ShapeDtypeStruct(own.shape, jnp.bfloat16),
        in_specs=[
            pl.BlockSpec((step, padded, RING), lambda i: (i, 0, 0)),
            pl.BlockSpec((step // 2, padded, TILE), lambda i: (i, 0, 0)),
            whole,
            whole,
        ],
        out_specs=pl.BlockSpec((step, padded, RING), lambda i: (i, 0, 0)),
        compiler_params=pltpu.CompilerParams(vmem_limit_bytes=VMEM_LIMIT),
        cost_estimate=pl.CostEstimate(
            flops=own.size * 4, bytes_accessed=own.size * 7, transcendentals=0
        ),
        name="blend",
    )(own, up, down, inv)


def turn(tiles, forward, lane):
    low, high = tiles
    shift, at = (1, 0) if forward else (TILE - 1, TILE - 1)
    low, high = pltpu.roll(low, shift, 1), pltpu.roll(high, shift, 1)
    return jnp.where(lane == at, high, low), jnp.where(lane == at, low, high)


def dice_kernel(prob_ref, label_ref, sums_ref, edge_ref, numer_ref, denom_ref):
    padded = prob_ref.shape[1]
    rows = prob_ref.shape[0] - 4
    groups = [(at, min(16, padded - at)) for at in range(0, padded, 16)]

    def tiles_of(ref, row, group):
        at, size = group
        return [ref[row, at : at + size, i * TILE : (i + 1) * TILE] for i in range(2)]

    def lanes(size):
        return lax.broadcasted_iota(jnp.int32, (size, TILE), 1)

    @pl.loop(0, rows + 2)
    def _(row):
        for group in groups:
            at, size = group
            centre = tiles_of(prob_ref, row + 1, group)
            before, after = tiles_of(prob_ref, row, group), tiles_of(prob_ref, row + 2, group)
            left, right = turn(centre, True, lanes(size)), turn(centre, False, lanes(size))
            for i in range(2):
                low = jnp.minimum(
                    jnp.minimum(before[i], after[i]), jnp.minimum(left[i], right[i])
                )
                edge_ref[row, at : at + size, i * TILE : (i + 1) * TILE] = centre[
                    i
                ] - jnp.minimum(centre[i], low)

    numer_ref[...] = jnp.zeros_like(numer_ref)
    denom_ref[...] = jnp.zeros_like(denom_ref)

    @pl.loop(0, rows)
    def _(row):
        def labels_of(at):
            line = label_ref[pl.ds(at, 1), :]
            return [line[:, i * TILE : (i + 1) * TILE] for i in range(2)]

        middle = labels_of(row + 1)
        line = lanes(1)
        near = (labels_of(row), labels_of(row + 2), turn(middle, True, line), turn(middle, False, line))
        near = [[other[i].astype(jnp.bfloat16) for i in range(2)] for other in near]
        middle = [middle[i].astype(jnp.bfloat16) for i in range(2)]
        for group in groups:
            at, size = group
            klass = (
                lax.broadcasted_iota(jnp.int32, (size, TILE), 0) + (1 + at)
            ).astype(jnp.float32).astype(jnp.bfloat16)
            lane = lanes(size)
            zero = jnp.zeros((size, TILE), jnp.bfloat16)
            centre = tiles_of(edge_ref, row + 1, group)
            before, after = tiles_of(edge_ref, row, group), tiles_of(edge_ref, row + 2, group)
            left, right = turn(centre, True, lane), turn(centre, False, lane)
            numer = numer_ref[at : at + size, :]
            denom = denom_ref[at : at + size, :]
            for i in range(2):
                wide = jnp.maximum(
                    jnp.maximum(centre[i], jnp.maximum(before[i], after[i])),
                    jnp.maximum(left[i], right[i]),
                )
                here = middle[i] == klass
                about = here
                for other in near:
                    about = about | (other[i] == klass)
                value = jnp.where(about, centre[i], zero).astype(jnp.float32)
                value = value + jnp.where(here, wide, zero).astype(jnp.float32)
                total = centre[i].astype(jnp.float32) + jnp.where(here, zero + 1, zero).astype(
                    jnp.float32
                )
                if i == 1:
                    value = jnp.where(lane < 64, value, 0.0)
                    total = jnp.where(lane < 64, total, 0.0)
                numer = numer + value
                denom = denom + total
            numer_ref[at : at + size, :] = numer
            denom_ref[at : at + size, :] = denom

    sums_ref[0] = jnp.broadcast_to(
        jnp.sum(numer_ref[...], axis=1, keepdims=True), (padded, TILE)
    )
    sums_ref[1] = jnp.broadcast_to(
        jnp.sum(denom_ref[...], axis=1, keepdims=True), (padded, TILE)
    )


def dice_of(prob, label):
    rows, padded, _ = prob.shape
    whole = pl.BlockSpec(memory_space=pltpu.VMEM)
    return pl.pallas_call(
        dice_kernel,
        out_shape=jax.ShapeDtypeStruct((2, padded, TILE), jnp.float32),
        in_specs=[whole] * 2,
        out_specs=whole,
        scratch_shapes=[
            pltpu.VMEM((rows - 2, padded, RING), jnp.bfloat16),
            pltpu.VMEM((padded, TILE), jnp.float32),
            pltpu.VMEM((padded, TILE), jnp.float32),
        ],
        compiler_params=pltpu.CompilerParams(vmem_limit_bytes=VMEM_LIMIT),
        cost_estimate=pl.CostEstimate(
            flops=prob.size * 30, bytes_accessed=prob.size * 2, transcendentals=0
        ),
        name="dice",
    )(prob, label)


def emit_kernel(chunks, *refs):
    prob_refs = refs[: len(chunks)]
    out_ref, turned_ref, sems = refs[-3:]
    _, span_y, classes = out_ref.shape
    span_x = out_ref.shape[0]

    copies = []
    base = 0
    for prob_ref, (first, rows) in zip(prob_refs, chunks):
        for i, at in enumerate((first, span_x - first - rows)):

            @pl.loop(0, rows)
            def _(index):
                for j in range(2):
                    block = prob_ref[i * rows + index, :, j * TILE : (j + 1) * TILE]
                    block = jnp.transpose(block.astype(jnp.float32), (1, 0))
                    stop = min((j + 1) * TILE, span_y)
                    turned_ref[base + index, j * TILE : stop, :] = block[
                        : stop - j * TILE, :classes
                    ].astype(jnp.bfloat16)

            copy = pltpu.make_async_copy(
                turned_ref.at[pl.ds(base, rows)], out_ref.at[pl.ds(at, rows)], sems.at[len(copies)]
            )
            copy.start()
            copies.append(copy)
            base += rows
    for copy in copies:
        copy.wait()


def emit(probs, chunks, shape, *before):
    anywhere = pl.BlockSpec(memory_space=pl.ANY)
    rows = sum(prob.shape[0] for prob in probs)
    size = sum(prob.size for prob in probs)
    return pl.pallas_call(
        functools.partial(emit_kernel, chunks),
        out_shape=jax.ShapeDtypeStruct(shape, probs[0].dtype),
        in_specs=[pl.BlockSpec(memory_space=pltpu.VMEM)] * len(probs) + [anywhere] * len(before),
        out_specs=anywhere,
        input_output_aliases={len(probs): 0} if before else {},
        scratch_shapes=[
            pltpu.VMEM((rows,) + shape[1:], probs[0].dtype),
            pltpu.SemaphoreType.DMA((2 * len(chunks),)),
        ],
        compiler_params=pltpu.CompilerParams(vmem_limit_bytes=VMEM_LIMIT),
        cost_estimate=pl.CostEstimate(
            flops=size * 4, bytes_accessed=size * 4, transcendentals=0
        ),
        name="emit",
    )(*probs, *before)


def shifted(block, axis, by):
    devices = lax.axis_size(axis)
    pairs = [(i, i + by) for i in range(devices) if 0 <= i + by < devices]
    return lax.ppermute(block, axis, pairs)


def gauss_line():
    position = jnp.arange(PATCH, dtype=jnp.float32) - (PATCH - 1) / 2.0
    sigma = 0.125 * PATCH
    return position * position / (2.0 * sigma * sigma)


def gauss_table():
    line = gauss_line()
    table = jnp.exp(-(line[:, None] + line[None, :]))
    return jnp.pad(table, ((0, QUAD), (0, TILE - PATCH)))


def three_parts(values):
    high = values.astype(jnp.bfloat16)
    rest = values - high.astype(jnp.float32)
    middle = rest.astype(jnp.bfloat16)
    low = (rest - middle.astype(jnp.float32)).astype(jnp.bfloat16)
    return jnp.stack([high, middle, low], axis=1)


def head_matrix(out_weight, out_bias):
    classes, feat = out_weight.shape
    matrix = jnp.concatenate(
        [out_weight, three_parts(out_bias), jnp.zeros((classes, 13), jnp.bfloat16)], axis=1
    )
    return jnp.concatenate([matrix, matrix[-2:]], axis=0)


def ring_of(plane):
    gap = jnp.zeros((plane.shape[0], RING - plane.shape[1]), plane.dtype)
    return jnp.concatenate([plane[:, 2:], gap, plane[:, :2]], axis=1)


def rows_of(plane, first, rows):
    span = plane.shape[0]
    return jnp.concatenate(
        [plane[first : first + rows], plane[span - first - rows : span - first]], axis=0
    )


def on_device(features, patch_ids, patch_count, labels, mlp_weight, mlp_bias, out_weight, out_bias):
    wide, narrow = lax.axis_size("wide"), lax.axis_size("narrow")
    here_wide, here_narrow = lax.axis_index("wide"), lax.axis_index("narrow")
    feat = features.shape[3]
    slots = features.shape[2]
    classes = out_weight.shape[0]
    span_x, span_y = labels.shape
    rows_q = ROWS * narrow
    feats = features[0, 0]

    slot_ids = jnp.arange(slots, dtype=jnp.int32)
    halves = jnp.arange(2, dtype=jnp.int32)
    columns = jnp.arange(2 * wide, dtype=jnp.int32)
    listed = slot_ids < patch_count[0, 0]
    column_of = patch_ids[0, 0][:, None] // rows_q + halves[None, :]
    hit = listed[:, None, None] & (column_of[:, :, None] == columns[None, None, :])
    pick = jnp.max(
        jnp.where(hit, (2 * slot_ids[:, None] + halves[None, :])[:, :, None], -1), axis=(0, 1)
    )

    def exchange(chunk, *after):
        payload = pack(feats, pick, *CHUNKS[chunk], *after)
        shape = payload.shape
        payload = payload.reshape((wide, 2) + shape[1:])
        return lax.all_to_all(payload, "wide", 0, 0, tiled=True).reshape(shape)

    received = [exchange(0), exchange(1)]

    kind = (patch_ids[0, 0] % rows_q - ROWS * here_narrow)[:, None] * 2 + halves[None, :]
    tag = jnp.max(jnp.where(hit, kind[:, :, None], -1), axis=(0, 1)).reshape(wide, 2)
    marked = labels + 1
    others = jnp.arange(wide, dtype=jnp.int32)[:, None]
    edges = jnp.where(others == here_wide + 1, marked[span_x - 2 :].reshape(1, -1), 0)
    edges = jnp.where(others == here_wide - 1, marked[:2].reshape(1, -1), edges)
    notes = lax.all_to_all(
        jnp.concatenate([tag, edges], axis=1), "wide", 0, 0, tiled=True
    )
    tag = notes[:, :2].reshape(-1)

    def rows_from(device):
        return jnp.sum(jnp.where(others == device, notes[:, 2:], 0), axis=0).reshape(2, span_y)

    label_wide = jnp.concatenate(
        [rows_from(here_wide - 1), marked, rows_from(here_wide + 1)], axis=0
    )
    valid = tag >= 0
    order = jnp.cumsum(valid.astype(jnp.int32)) - 1
    code = jnp.where(valid, columns * 8 + tag, 0)
    place = valid[:, None] & (order[:, None] == columns[None, :])
    codes = jnp.concatenate(
        [
            jnp.sum(jnp.where(place, code[:, None], 0), axis=0),
            jnp.sum(valid.astype(jnp.int32))[None],
        ]
    )

    table = gauss_table()
    square = table[:PATCH, :PATCH].reshape(2, QUAD, PATCH)
    kinds = jnp.arange(2 * ROWS, dtype=jnp.int32)
    counts = jnp.sum((tag.reshape(wide, 2, 1) == kinds).astype(jnp.float32), axis=0)

    def beside(columns, by):
        block = jnp.concatenate(
            [columns.astype(jnp.float32), counts.reshape(2 * ROWS, 2)], axis=0
        )
        return shifted(block, "narrow", by)

    def parts_of(block):
        return block[:-2 * ROWS].astype(jnp.int32), block[-2 * ROWS :].reshape(2, 2 * ROWS)

    blocks = beside(label_wide[:, span_y - 2 :], 1), beside(label_wide[:, :2], -1)
    head_weight = head_matrix(out_weight, out_bias)
    bias_tile = jnp.broadcast_to(mlp_bias[:, None], (feat, TILE))

    def head_at(chunk):
        return head_of(
            received[chunk], codes, mlp_weight, bias_tile, head_weight,
            table[:, :PATCH].reshape(-1, 3, 1, TILE), *CHUNKS[chunk], classes
        )

    heads = []
    for chunk in range(len(CHUNKS) - 1):
        heads.append(head_at(chunk))
        if chunk + 2 < len(CHUNKS):
            received.append(exchange(chunk + 2, heads[chunk][2]))
    _, low_block, high_block = lax.optimization_barrier((heads[1][2],) + blocks)
    label_low, counts_low = parts_of(low_block)
    label_high, counts_high = parts_of(high_block)

    def plane_of(counts, row):
        pairs = counts.reshape(2, ROWS, 2)[:, row, :, None, None]
        return jnp.sum(pairs * square[None], axis=1).reshape(span_x, PATCH)

    norm = sum(
        jnp.pad(plane_of(counts, i), ((0, 0), (QUAD * i, QUAD * (ROWS - 1 - i))))
        for i in range(ROWS)
    )
    came = plane_of(counts_low, 3)
    norm = jnp.concatenate(
        [
            came[:, 46:48] + plane_of(counts_low, 2)[:, 94:96],
            norm[:, :QUAD] + came[:, 48:],
            norm[:, QUAD:span_y],
            norm[:, span_y : span_y + 2] + plane_of(counts_high, 0)[:, :2],
        ],
        axis=1,
    )
    across = ROWS * QUAD * here_narrow - 2 + jnp.arange(span_y + 4, dtype=jnp.int32)
    inside = (across >= 0) & (across < narrow * span_y)
    inverse = ring_of(jnp.where(inside[None, :], 1.0 / (norm + 0.001), 0.0))

    label_wide = jnp.concatenate([label_low, label_wide, label_high], axis=1)
    centre = label_wide[1:-1, 1:-1]
    same = (
        (label_wide[:-2, 1:-1] == centre)
        & (label_wide[2:, 1:-1] == centre)
        & (label_wide[1:-1, :-2] == centre)
        & (label_wide[1:-1, 2:] == centre)
    )
    boundary = jnp.where(same, 0, centre)
    boundary = ring_of(jnp.pad(boundary, ((0, 0), (1, 1))))

    probs = []
    for chunk, (first, rows) in enumerate(CHUNKS):
        own, up, down = heads[chunk] if chunk + 1 < len(CHUNKS) else head_at(chunk)
        up = shifted(up, "narrow", 1)
        down = shifted(down, "narrow", -1)
        prob = blend_of(own, up, down, rows_of(inverse, first, rows))
        probs.append(prob)
    edge_rows = CHUNKS[0][1]
    before = shifted(probs[0][2 * edge_rows - 2 :], "wide", 1)
    after = shifted(probs[0][:2], "wide", -1)
    last, last_rows = CHUNKS[-1]
    lows = [prob[:rows] for prob, (_, rows) in zip(probs, CHUNKS)]
    highs = [prob[rows:] for prob, (_, rows) in zip(probs, CHUNKS)]
    low = jnp.concatenate([before] + lows[:-1], axis=0)
    high = jnp.concatenate(highs[:-1][::-1] + [after], axis=0)
    middle = jnp.concatenate([lows[-2][-4:], probs[-1], highs[-2][:4]], axis=0)
    sums = (
        dice_of(low, boundary[:last])
        + dice_of(high, boundary[span_x - last + 2 :])
        + dice_of(middle, boundary[last - 2 : span_x - last + 4])
    )[:, :, 0]
    shape = (span_x, span_y, classes)
    blended = emit(probs[:-1], CHUNKS[:-1], shape)
    blended = emit(probs[-1:], CHUNKS[-1:], shape, blended)
    whole = jnp.broadcast_to(sums[None], (wide * narrow,) + sums.shape)
    whole = jnp.sum(lax.all_to_all(whole, ("wide", "narrow"), 0, 0, tiled=True), axis=0)
    dice = ((whole[0] + 1.0) / (whole[1] + 1.0))[:classes]
    slab_sums = (sums[:, :classes] / jnp.float32(span_x)).reshape(1, 1, 2, classes)
    return (blended.transpose(2, 0, 1), dice, slab_sums)


def solution(mesh):
    return jax.shard_map(
        on_device,
        mesh=mesh,
        in_specs=(
            P("wide", "narrow", None, None, None),
            P("wide", "narrow", None),
            P("wide", "narrow"),
            P("wide", "narrow"),
            P(),
            P(),
            P(),
            P(),
        ),
        out_specs=(P(None, "wide", "narrow"), P(), P("wide", "narrow", None, None)),
        check_vma=False,
    )
```
